128 devices in a mesh: tm: 8 (over z, core), space: 16 (over x, y).
Axes of the slice: x: 4, y: 4, z: 4, core: 2. Of those that a mesh axis runs over, the one named last changes fastest.
Arguments:
- increment: float32 [16, 4, 256, 1440], P('tm', None, 'space'), may hold values from -4 to 4
- forcing: float32 [16, 4, 256, 1440], P('tm', None, 'space'), may hold values from -4 to 4
- lat_courant: float32 [4, 256, 1440], P(None, 'space'), may hold values from 0.05 to 0.45
- lon_courant: float32 [4, 256, 1440], P(None, 'space'), may hold values from 0.05 to 0.45
- error_weight: float32 [4, 256, 1440], P(None, 'space'), may hold values from 0.5 to 4
- site_index: int32 [16, 4, 32768], P('tm', None, 'space'), may hold values from 0 to 92159
- site_count: int32 [16, 4, 16], P('tm', None, 'space'), may hold values from 1024 to 2048, as said below
- site_value: float32 [16, 4, 32768], P('tm', None, 'space'), may hold values from -6 to 6
- site_weight: float32 [16, 4, 32768], P('tm', None, 'space'), may hold values from 0.5 to 4
- pair_step: bfloat16 [8, 16, 4, 256, 1440], P(None, 'tm', None, 'space'), may hold values from -24 to 24
- pair_change: bfloat16 [8, 16, 4, 256, 1440], P(None, 'tm', None, 'space'), may hold values from -108 to 108, as said below
Outputs:
- gradient: float32 [16, 4, 256, 1440], P('tm', None, 'space')
- direction: float32 [16, 4, 256, 1440], P('tm', None, 'space')
The draws below stay inside these ranges and needn't reach their ends.
Inputs may be any that keep to these rules, and one draw needn't show every extreme that they name: `site_count`: in every step and sub-window some tile has all 2048 slots live, and every tile at least half of them. `pair_change`: each entry has the sign of the matching entry of pair_step, so that <y_i, s_i> > 0.
All inputs are finite; a program needn't handle non-finite values.
Results may differ from the reference program's by a relative error of at most 0.0003.
Values sent between devices are 32-bit elements; how exact they have to be, the bound alone decides.
No kernel may reach another device: no remote copies, remote signals or barrier semaphores. Data moves between devices by JAX's collectives and lax.ppermute only.
A program may use at most 128 MiB of HBM per device.

```python
import math
import jax
import jax.numpy as jnp

LV = 4
ROWS = 16
NLON = 1440
NSTEP = 4
PAIRS = 8
OBS_TILE = 2048
SUBWIN = 16
TILES = 16
NLAT = 256
NOBS = 32768


def pattern(key):
    key = jax.random.fold_in(key, 3)
    first = jax.random.fold_in(key, 0)
    shape = (SUBWIN, LV, NLAT, NLON)
    gauss = jax.random.truncated_normal(first, -4.0, 4.0, shape, jnp.float32)
    return gauss


def pair_base(key):
    common = pattern(key)
    key = jax.random.fold_in(key, 5)
    first = jax.random.fold_in(key, 0)
    third = jax.random.fold_in(key, 2)
    fourth = jax.random.fold_in(key, 3)
    fifth = jax.random.fold_in(key, 4)
    shape = (PAIRS, SUBWIN, LV, NLAT, NLON)
    gauss = jax.random.truncated_normal(first, -4.0, 4.0, shape, jnp.float32)
    noise = gauss
    weight_size = jax.random.uniform(third, (PAIRS, 1, 1, 1, 1), jnp.float32, 0.4, 1.0)
    flip = jnp.where(jax.random.uniform(fourth, (PAIRS, 1, 1, 1, 1), jnp.float32) < 0.5, -1.0, 1.0)
    rise = 1.0 + 2.0 * jnp.arange(NLAT, dtype=jnp.float32)[:, None] / NLAT
    level = jnp.exp(jax.random.uniform(fifth, (PAIRS, SUBWIN, LV, 1, 1), jnp.float32, -0.7, 0.7))
    return jnp.clip((weight_size * flip * common[None] + noise) * rise * level, -24.0, 24.0)


def draw_increment(key, part):
    return pattern(key)


def draw_pair_step(key, part):
    return pair_base(key).astype(jnp.bfloat16)


def draw_pair_change(key, part):
    base = pair_base(key)
    key = jax.random.fold_in(key, 7)
    first, second, third = jax.random.split(key, 3)
    factor = jnp.exp(jax.random.uniform(first, base.shape, jnp.float32, -0.5, 0.5))
    coarse = jnp.exp(jax.random.uniform(second, (PAIRS, SUBWIN, LV, 1, 1), jnp.float32, -0.5, 0.5))
    overall = jnp.exp(jax.random.uniform(third, (PAIRS, 1, 1, 1, 1), jnp.float32, -0.5, 0.5))
    return (base * factor * coarse * overall).astype(jnp.bfloat16)


def draw_site_count(key, part):
    key = jax.random.fold_in(key, 11)
    first, second = jax.random.split(key)
    base = jax.random.randint(first, (SUBWIN, NSTEP, TILES), OBS_TILE // 2, OBS_TILE + 1)
    pick = jax.random.randint(second, (SUBWIN, NSTEP, 1), 0, TILES)
    tiles = jnp.arange(TILES, dtype=jnp.int32)[None, None, :]
    return jnp.where(tiles == pick, OBS_TILE, base).astype(jnp.int32)


def touch_ends(entries, rng, low, largest):
    longest = entries.shape.index(max(entries.shape))
    spots = []
    for shift in (0, 1):
        where = [jax.random.randint(jax.random.fold_in(rng, axis), (), 0, length) for axis, length in enumerate(entries.shape)]
        where[longest] = (where[longest] + shift) % entries.shape[longest]
        spots.append(tuple(where))
    return entries.at[spots[0]].set(low).at[spots[1]].set(largest)


def steps_of(stream_key, shape, pieces, least, top_value):
    def one(dim, shards_of):
        draws = jax.random.uniform(jax.random.fold_in(jax.random.fold_in(stream_key, 6), dim), (shards_of,), jnp.float32, least / len(pieces), top_value / len(pieces))
        return jnp.repeat(jnp.exp(draws), shape[dim] // shards_of).reshape((-1,) + (1,) * (len(shape) - dim - 1))

    level = one(*pieces[0])
    for cut in pieces[1:]:
        level = level * one(*cut)
    return level


def gaussian(key, dims, deviation, bound, shards=(), kind=jnp.bfloat16):
    values = deviation * jax.random.normal(key, dims, jnp.float32)
    if shards:
        values = values * steps_of(key, dims, shards, -0.22, 0.18)
    return jnp.clip(values, -bound, bound).astype(kind)


def setup_inputs(seed: int = 0) -> dict:
    key_of = jax.random.split(jax.random.key(seed), 12)
    increment = draw_increment(jax.random.fold_in(key_of[11], 71), 0)
    forcing = gaussian(key_of[1], (SUBWIN, LV, NLAT, NLON), 0.3, 4.0, ((0, 8), (2, 16)), jnp.float32)
    lat_courant = jnp.clip(0.05 + 0.39999999 * jax.random.uniform(key_of[2], (LV, NLAT, NLON), jnp.float32) ** steps_of(key_of[2], (LV, NLAT, NLON), ((1, 16),), -0.2, 0.2), 0.05, 0.45)
    lon_courant = jnp.clip(0.05 + 0.39999999 * jax.random.uniform(key_of[3], (LV, NLAT, NLON), jnp.float32) ** steps_of(key_of[3], (LV, NLAT, NLON), ((1, 16),), -0.2, 0.2), 0.05, 0.45)
    error_weight = jnp.clip(jnp.exp(math.log(4.0) - 2.0794415 * jax.random.uniform(key_of[4], (LV, NLAT, NLON), jnp.float32) ** steps_of(key_of[4], (LV, NLAT, NLON), ((1, 16),), -0.2, 0.2)), 0.5, 4.0)
    site_index = touch_ends(jax.random.randint(key_of[5], (SUBWIN, NSTEP, NOBS), 0, LV * ROWS * NLON), jax.random.fold_in(key_of[5], 1), 0, (LV * ROWS * NLON) - 1).astype(jnp.int32)
    site_count = draw_site_count(jax.random.fold_in(key_of[11], 71), 0)
    site_value = gaussian(key_of[7], (SUBWIN, NSTEP, NOBS), 1.0, 6.0, ((0, 8), (2, 16)), jnp.float32)
    site_weight = jnp.clip(jnp.exp(math.log(4.0) - 2.0794415 * jax.random.uniform(key_of[8], (SUBWIN, NSTEP, NOBS), jnp.float32) ** steps_of(key_of[8], (SUBWIN, NSTEP, NOBS), ((0, 8), (2, 16)), -0.2, 0.2)), 0.5, 4.0)
    pair_step = draw_pair_step(jax.random.fold_in(key_of[11], 71), 0)
    pair_change = draw_pair_change(jax.random.fold_in(key_of[11], 71), 0)
    return dict(increment=increment, forcing=forcing, lat_courant=lat_courant, lon_courant=lon_courant, error_weight=error_weight, site_index=site_index, site_count=site_count, site_value=site_value, site_weight=site_weight, pair_step=pair_step, pair_change=pair_change)


def tangent(state, lat_courant, lon_courant, forcing):
    above = jnp.concatenate([jnp.zeros_like(state[..., :1, :]), state[..., :-1, :]], axis=-2)
    left = jnp.roll(state, 1, axis=-1)
    return (1.0 - lat_courant - lon_courant) * state + lat_courant * above + lon_courant * left + forcing


def adjoint(dual, lat_courant, lon_courant):
    lat_part = lat_courant * dual
    below = jnp.concatenate([lat_part[..., 1:, :], jnp.zeros_like(lat_part[..., :1, :])], axis=-2)
    right = jnp.roll(lon_courant * dual, -1, axis=-1)
    return (1.0 - lat_courant - lon_courant) * dual + below + right


def inject(weights, cells, total):
    def one(values, where):
        return jnp.zeros((total,), jnp.float32).at[where].add(values)
    return jax.vmap(one)(weights, cells)


def inner(left, right):
    return jnp.sum(left * right)


def reference(increment, forcing, lat_courant, lon_courant, error_weight, site_index, site_count, site_value, site_weight, pair_step, pair_change):
    column = jnp.arange(NOBS, dtype=jnp.int32)
    tile = column // OBS_TILE
    level = site_index // (ROWS * NLON)
    within = site_index % (ROWS * NLON)
    cells = level * (NLAT * NLON) + (tile[None, None, :] * ROWS + within // NLON) * NLON + within % NLON
    live = (column % OBS_TILE)[None, None, :] < jnp.repeat(site_count, OBS_TILE, axis=2)
    total = LV * NLAT * NLON
    state = increment
    deps = []
    for step in range(NSTEP):
        state = tangent(state, lat_courant, lon_courant, forcing)
        seen = jnp.take_along_axis(state.reshape(SUBWIN, total), cells[:, step], axis=1)
        deps.append(jnp.where(live[:, step], site_weight[:, step] * (site_value[:, step] - seen), 0.0))
    previous = jnp.concatenate([jnp.zeros_like(state[:1]), state[:-1]], axis=0)
    weighted = error_weight * (increment - previous)
    dual = jnp.concatenate([weighted[1:], jnp.zeros_like(weighted[:1])], axis=0)
    for step in range(NSTEP - 1, -1, -1):
        dual = dual + inject(deps[step], cells[:, step], total).reshape(dual.shape)
        dual = adjoint(dual, lat_courant, lon_courant)
    gradient = weighted - dual
    rhos = [1.0 / inner(pair_change[i].astype(jnp.float32), pair_step[i].astype(jnp.float32)) for i in range(PAIRS)]
    newest = pair_change[PAIRS - 1].astype(jnp.float32)
    gamma = inner(pair_step[PAIRS - 1].astype(jnp.float32), newest) / inner(newest, newest)
    vector = gradient
    alphas = [None] * PAIRS
    for i in range(PAIRS - 1, -1, -1):
        alphas[i] = rhos[i] * inner(pair_step[i].astype(jnp.float32), vector)
        vector = vector - alphas[i] * pair_change[i].astype(jnp.float32)
    result = gamma * vector
    for i in range(PAIRS):
        beta = rhos[i] * inner(pair_change[i].astype(jnp.float32), result)
        result = result + (alphas[i] - beta) * pair_step[i].astype(jnp.float32)
    return gradient, result
```

```python
import functools

import jax
import jax.numpy as jnp
from jax import lax
from jax.experimental import pallas as pl
from jax.experimental.pallas import tpu as pltpu
from jax.sharding import PartitionSpec as P

NSTEP = 4
LANES = 128
F32 = jnp.float32
BF16 = jnp.bfloat16
WHOLE = pl.BlockSpec(memory_space=pltpu.VMEM)
SCALAR = pl.BlockSpec(memory_space=pltpu.SMEM)


def shifted(shard, axis, by):
    count = lax.axis_size(axis)
    pairs = [(i, i + by) for i in range(count) if 0 <= i + by < count]
    return lax.ppermute(shard, axis, pairs)


def west(x):
    return jnp.concatenate([x[:, -1:], x[:, :-1]], axis=1)


def east(x):
    return jnp.concatenate([x[:, 1:], x[:, :1]], axis=1)


def rows_of(x):
    return lax.broadcasted_iota(jnp.int32, x.shape, 0)


def params(mib):
    return pltpu.CompilerParams(vmem_limit_bytes=mib << 20)


def halves(x):
    high = x.astype(BF16)
    return high, (x - high.astype(F32)).astype(BF16)


def edge_kernel(inc_ref, forcing_ref, lat_ref, lon_ref, out_ref):
    levels = lat_ref.shape[0]
    for j in range(out_ref.shape[0]):
        sub, lev = divmod(j, levels)
        x = inc_ref[sub, lev]
        lat, lon, push = lat_ref[lev], lon_ref[lev], forcing_ref[sub, lev]
        rest = 1.0 - lat - lon
        for step in range(NSTEP):
            out_ref[j, step : step + 1, :] = x[7:8, :]
            if step < NSTEP - 1:
                x = rest * x + lat * pltpu.roll(x, 1, 0) + lon * west(x) + push


def pairs_kernel(step_ref, change_ref, out_ref, acc_ref):
    block = pl.program_id(0)
    pairs, _, _, rows, longs = step_ref.shape
    both = 2 * pairs * rows

    @pl.when(block == 0)
    def _():
        acc_ref[...] = jnp.zeros_like(acc_ref)

    for lev in range(step_ref.shape[2]):
        steps = step_ref[:, 0, lev].reshape(pairs * rows, longs)
        changes = change_ref[:, 0, lev].reshape(pairs * rows, longs)
        left = jnp.concatenate([steps, changes], axis=0)
        acc_ref[...] += lax.dot_general(
            left, changes, (((1,), (1,)), ((), ())), preferred_element_type=F32
        )

    @pl.when(block == pl.num_programs(0) - 1)
    def _():
        total = acc_ref[...]
        row = lax.broadcasted_iota(jnp.int32, total.shape, 0)
        col = lax.broadcasted_iota(jnp.int32, total.shape, 1)
        total = jnp.where(row % rows == col % rows, total, 0.0)
        sums = [
            jnp.sum(total[v * rows : (v + 1) * rows], axis=0, keepdims=True)
            for v in range(both // rows)
        ]
        out_ref[...] = jnp.concatenate(sums, axis=0)


def observe_kernel(
    last_ref,
    inc_ref,
    forcing_ref,
    lat_ref,
    lon_ref,
    ew_ref,
    next_ref,
    above_ref,
    index_ref,
    count_ref,
    value_ref,
    weight_ref,
    end_ref,
    edge_ref,
    inject_ref,
    cell_ref,
    lane_ref,
    dep_ref,
    state_ref,
    hot_ref,
    value_row,
    weight_row,
    live_row,
):
    subs, levels, rows, longs = inc_ref.shape
    slots = index_ref.shape[2]
    tiles = -(-longs // LANES)
    half = tiles * levels * 8
    wide = tiles * LANES
    state_ref[:, :, :, longs - longs % LANES :] = jnp.zeros(
        (subs * NSTEP, levels, rows, LANES), F32
    )

    def tangent(j, _):
        sub, lev = j // levels, j % levels
        x = inc_ref[sub, lev]
        lat, lon, push = lat_ref[lev], lon_ref[lev], forcing_ref[sub, lev]
        rest = 1.0 - lat - lon
        top = rows_of(x) == 0
        for step in range(NSTEP):
            above = jnp.where(top, above_ref[j, step : step + 1, :], pltpu.roll(x, 1, 0))
            x = rest * x + lat * above + lon * west(x) + push
            state_ref[sub * NSTEP + step, lev, :, :longs] = x
        end_ref[sub, lev] = x
        return 0

    lax.fori_loop(0, subs * levels, tangent, 0)

    slot = lax.broadcasted_iota(jnp.int32, (1, slots), 1)
    for sub in range(subs):
        index = index_ref[sub]
        row = ((index.astype(F32) + 0.5) * (1.0 / longs)).astype(jnp.int32)
        lon = index - row * longs
        lat = row % rows
        cell = (lat // 8) * half + (lon // LANES) * (levels * 8) + (row // rows) * 8 + lat % 8
        lane = lon % LANES
        value, weight = value_ref[sub], weight_ref[sub]
        for step in range(NSTEP):
            k = sub * NSTEP + step
            cell_ref[k] = cell[step : step + 1]
            lane_ref[k] = lane[step : step + 1]
            value_row[k] = value[step : step + 1]
            weight_row[k] = weight[step : step + 1]
            live_row[k] = (slot < count_ref[sub, step]).astype(F32)

    def one(k, _):
        cell = cell_ref[k].astype(jnp.int16)
        lane = lane_ref[k].astype(jnp.int16)
        blocks = []
        for first in range(0, 2 * tiles, 4):
            part = []
            for at in range(first, first + 4):
                lower, tile = divmod(at, tiles)
                part.append(
                    state_ref[
                        k, :, lower * 8 : lower * 8 + 8, tile * LANES : (tile + 1) * LANES
                    ].reshape(levels * 8, LANES)
                )
            blocks.append(jnp.concatenate(part, axis=0).T)
        table = jnp.concatenate(halves(jnp.concatenate(blocks, axis=1)), axis=0)
        chunk = 256
        seen = []
        place = lax.broadcasted_iota(jnp.int16, (LANES, chunk), 0)
        for first in range(0, slots, chunk):
            part = slice(first, first + chunk)
            hot = jnp.where(
                lax.broadcasted_iota(jnp.int16, (2 * half, chunk), 0) == cell[:, part],
                jnp.ones((), BF16),
                jnp.zeros((), BF16),
            )
            hot_ref[:, part] = hot[:half]
            got = jnp.dot(table, hot, preferred_element_type=F32)
            got = got[:LANES] + got[LANES:]
            mine = lax.broadcasted_iota(jnp.int32, (LANES, chunk), 0) == lane_ref[k][:, part]
            seen.append(jnp.sum(jnp.where(mine, got, 0.0), axis=0, keepdims=True))
        seen = jnp.concatenate(seen, axis=1)
        dep = jnp.where(live_row[k] > 0.0, weight_row[k] * (value_row[k] - seen), 0.0)
        dep_ref[k] = dep
        inject_ref[k] = spread(hot_ref[...], lane, dep, levels, longs)
        return 0

    lax.fori_loop(0, subs * NSTEP, one, 0)

    for sub in range(subs):
        for lev in range(levels):
            j = sub * levels + lev
            later = next_ref[lev, :8] if sub == subs - 1 else inc_ref[sub + 1, lev, :8]
            d = ew_ref[lev, :8] * (later - end_ref[sub, lev, :8])
            if sub == subs - 1:
                d = d * last_ref[0]
            lat, lon = lat_ref[lev, :8], lon_ref[lev, :8]
            rest = 1.0 - lat - lon
            for step in range(NSTEP - 1, -1, -1):
                d = d + inject_ref[sub * NSTEP + step, lev]
                part = lat * d
                edge_ref[j, step : step + 1, :] = part[:1, :]
                if step:
                    d = rest * d + pltpu.roll(part, 7, 0) + east(lon * d)


def spread(hot, lane, dep, levels, longs):
    slots = dep.shape[1]
    high, low = halves(dep)
    mine = lax.broadcasted_iota(jnp.int16, (LANES, slots), 0) == lane
    zero = jnp.zeros((), BF16)
    values = jnp.concatenate([jnp.where(mine, high, zero), jnp.where(mine, low, zero)], axis=0)
    out = lax.dot_general(hot, values, (((1,), (1,)), ((), ())), preferred_element_type=F32)
    out = out[:, :LANES] + out[:, LANES:]
    band = levels * 8
    tiles = out.shape[0] // band
    parts = [out[t * band : (t + 1) * band] for t in range(tiles)]
    return jnp.concatenate(parts, axis=1)[:, :longs].reshape(levels, 8, longs)


def lower_kernel(cell_ref, lane_ref, dep_ref, inject_ref):
    count, levels, _, longs = inject_ref.shape
    slots = dep_ref.shape[2]
    half = -(-longs // LANES) * levels * 8

    def one(k, _):
        cell = (cell_ref[k] - half).astype(jnp.int16)
        hot = jnp.where(
            lax.broadcasted_iota(jnp.int16, (half, slots), 0) == cell,
            jnp.ones((), BF16),
            jnp.zeros((), BF16),
        )
        inject_ref[k] = spread(hot, lane_ref[k].astype(jnp.int16), dep_ref[k], levels, longs)
        return 0

    lax.fori_loop(0, count, one, 0)


def gradient_kernel(
    last_ref,
    inc_ref,
    lat_ref,
    lon_ref,
    ew_ref,
    next_ref,
    end_ref,
    previous_ref,
    upper_ref,
    lower_ref,
    below_ref,
    gram_ref,
    step_ref,
    change_ref,
    grad_ref,
    stats_ref,
    step_buf,
    change_buf,
    dots_ref,
    sems,
):
    subs, levels, rows, longs = inc_ref.shape
    pairs = step_ref.shape[0]
    count = subs * levels

    def copies(j):
        sub, lev = j // levels, j % levels
        return (
            pltpu.make_async_copy(step_ref.at[:, sub, lev], step_buf.at[j], sems.at[0, j]),
            pltpu.make_async_copy(change_ref.at[:, sub, lev], change_buf.at[j], sems.at[1, j]),
        )

    for j in range(count):
        for copy in copies(j):
            copy.start()
    dots_ref[...] = jnp.zeros_like(dots_ref)

    def one(j, _):
        sub, lev = j // levels, j % levels
        ew = ew_ref[lev]
        final = sub == subs - 1
        later = jnp.where(final, next_ref[lev], inc_ref[jnp.minimum(sub + 1, subs - 1), lev])
        d = ew * (later - end_ref[sub, lev])
        d = d * jnp.where(final, last_ref[0], 1.0)
        lat, lon = lat_ref[lev], lon_ref[lev]
        rest = 1.0 - lat - lon
        bottom = rows_of(d) == rows - 1
        for step in range(NSTEP - 1, -1, -1):
            k = sub * NSTEP + step
            d = d + jnp.concatenate([upper_ref[k, lev], lower_ref[k, lev]], axis=0)
            part = lat * d
            below = jnp.where(
                bottom, below_ref[j, step : step + 1, :], pltpu.roll(part, rows - 1, 0)
            )
            d = rest * d + below + east(lon * d)
        earlier = jnp.where(sub == 0, previous_ref[lev], end_ref[jnp.maximum(sub - 1, 0), lev])
        g = ew * (inc_ref[sub, lev] - earlier) - d
        grad_ref[sub, lev] = g
        for copy in copies(j):
            copy.wait()
        for i in range(pairs):
            for which, buf in enumerate((step_buf, change_buf)):
                dots_ref[which * pairs + i] += fold(g * buf[j, i].astype(F32))
        return 0

    lax.fori_loop(0, count, one, 0)
    sums = [jnp.sum(dots_ref[v], axis=0, keepdims=True) for v in range(2 * pairs)]
    sums = jnp.concatenate(sums, axis=0)
    dots = jnp.sum(sums, axis=1, keepdims=True)
    raw = gram_ref[...]
    row = lax.broadcasted_iota(jnp.int32, raw.shape, 0)
    col = lax.broadcasted_iota(jnp.int32, raw.shape, 1)
    group = col // rows
    here = col % rows == row
    out = jnp.zeros((1, raw.shape[1]), F32)
    for c in range(pairs):
        part = jnp.sum(jnp.where(group == c, raw, 0.0), axis=1, keepdims=True)
        out += jnp.sum(jnp.where(here & (group == c), part, 0.0), axis=0, keepdims=True)
    stats_ref[0:1, :] = out
    stats_ref[1:2, :] = jnp.sum(jnp.where(here, dots, 0.0), axis=0, keepdims=True)


def fold(x):
    longs = x.shape[1]
    whole = longs - longs % LANES
    x = x[:8] + x[8:]
    out = x[:, :LANES]
    for first in range(LANES, whole, LANES):
        out = out + x[:, first : first + LANES]
    if whole < longs:
        tail = jnp.concatenate(
            [x[:, whole:], jnp.zeros((8, LANES - (longs - whole)), F32)], axis=1
        )
        out = out + tail
    return out


def direction_kernel(stats_ref, grad_ref, step_ref, change_ref, out_ref, coef_ref):
    pairs = step_ref.shape[0]
    both = 2 * pairs

    @pl.when(pl.program_id(0) == 0)
    def _():
        gram = jnp.sum(stats_ref[:, 0, :], axis=0, keepdims=True)
        dots = jnp.sum(stats_ref[:, 1, :], axis=0, keepdims=True)
        shape = (both, LANES)
        row = lax.broadcasted_iota(jnp.int32, shape, 0)
        col = lax.broadcasted_iota(jnp.int32, shape, 1)
        group, inner = col // both, col % both
        gram = jnp.broadcast_to(gram, shape)
        dots = jnp.broadcast_to(dots, shape)

        def column(mask, x):
            return jnp.sum(jnp.where(mask, x, 0.0), axis=1, keepdims=True)

        dots = column((inner == row) & (group == 0), dots)
        by_change = [column((inner == row) & (group == c), gram) for c in range(pairs)]
        by_step = [column((group == row) & (inner == i), gram)[:pairs] for i in range(pairs)]
        diagonal = column((group == row) & (inner == row), gram)[:pairs]
        rho = 1.0 / diagonal
        with_step, with_change = dots[:pairs], dots[pairs:]
        alphas = [None] * pairs
        for i in range(pairs - 1, -1, -1):
            alphas[i] = rho[i : i + 1] * with_step[i : i + 1]
            with_step = with_step - alphas[i] * by_change[i][:pairs]
            with_change = with_change - alphas[i] * by_change[i][pairs:]
        gamma = diagonal[pairs - 1 : pairs] / by_change[pairs - 1][both - 1 : both]
        with_change = gamma * with_change
        coef_ref[both] = jnp.broadcast_to(gamma, (8, LANES))
        for i in range(pairs):
            beta = rho[i : i + 1] * with_change[i : i + 1]
            rise = alphas[i] - beta
            with_change = with_change + rise * by_step[i]
            coef_ref[i] = jnp.broadcast_to(rise, (8, LANES))
            coef_ref[pairs + i] = jnp.broadcast_to(-gamma * alphas[i], (8, LANES))

    gamma = coef_ref[both][:1, :1]
    for lev in range(step_ref.shape[2]):
        total = gamma * grad_ref[0, lev]
        for i in range(pairs):
            total += coef_ref[i][:1, :1] * step_ref[i, 0, lev].astype(F32)
            total += coef_ref[pairs + i][:1, :1] * change_ref[i, 0, lev].astype(F32)
        out_ref[0, lev] = total


def on_device(
    increment,
    forcing,
    lat_courant,
    lon_courant,
    error_weight,
    site_index,
    site_count,
    site_value,
    site_weight,
    pair_step,
    pair_change,
):
    subs, levels, rows, longs = increment.shape
    pairs = pair_step.shape[0]
    slots = site_index.shape[2]
    count = subs * levels
    tiles = -(-longs // LANES)
    half = tiles * levels * 8
    devices = lax.axis_size("tm") * lax.axis_size("space")
    last = jnp.where(lax.axis_index("tm") == lax.axis_size("tm") - 1, 0.0, 1.0)
    last = last.astype(F32).reshape(1)

    following = shifted(increment[0], "tm", -1)
    edge = pl.pallas_call(
        edge_kernel,
        grid=(1,),
        in_specs=[
            pl.BlockSpec((subs, levels, 8, longs), lambda i: (0, 0, 1, 0)),
            pl.BlockSpec((subs, levels, 8, longs), lambda i: (0, 0, 1, 0)),
            pl.BlockSpec((levels, 8, longs), lambda i: (0, 1, 0)),
            pl.BlockSpec((levels, 8, longs), lambda i: (0, 1, 0)),
        ],
        out_specs=pl.BlockSpec((count, NSTEP, longs), lambda i: (0, 0, 0)),
        out_shape=jax.ShapeDtypeStruct((count, NSTEP, longs), F32),
        compiler_params=params(16),
        name="edge",
    )(increment, forcing, lat_courant, lon_courant)
    above = shifted(edge, "space", 1)

    some = 2
    pair_spec = pl.BlockSpec(
        (pairs, 1, some, rows, longs), lambda b: (0, b // (levels // some), b % (levels // some), 0, 0)
    )
    blocks = count // some
    gram = pl.pallas_call(
        pairs_kernel,
        grid=(blocks,),
        in_specs=[pair_spec, pair_spec],
        out_specs=pl.BlockSpec((2 * pairs, pairs * rows), lambda b: (0, 0)),
        out_shape=jax.ShapeDtypeStruct((2 * pairs, pairs * rows), F32),
        scratch_shapes=[pltpu.VMEM((2 * pairs * rows, pairs * rows), F32)],
        compiler_params=params(16),
        cost_estimate=pl.CostEstimate(
            flops=2 * 256 * 128 * 184320, bytes_accessed=5898240, transcendentals=0
        ),
        name="pairs",
    )(pair_step, pair_change)

    row_shape = (subs * NSTEP, 1, slots)
    end, edge, upper, cell, lane, dep = pl.pallas_call(
        observe_kernel,
        in_specs=[SCALAR] + [WHOLE] * 8 + [SCALAR] + [WHOLE] * 2,
        out_specs=[WHOLE] * 6,
        out_shape=[
            jax.ShapeDtypeStruct(increment.shape, F32),
            jax.ShapeDtypeStruct((count, NSTEP, longs), F32),
            jax.ShapeDtypeStruct((subs * NSTEP, levels, 8, longs), F32),
            jax.ShapeDtypeStruct(row_shape, jnp.int32),
            jax.ShapeDtypeStruct(row_shape, jnp.int32),
            jax.ShapeDtypeStruct(row_shape, F32),
        ],
        scratch_shapes=[
            pltpu.VMEM((subs * NSTEP, levels, rows, tiles * LANES), F32),
            pltpu.VMEM((half, slots), BF16),
            pltpu.VMEM(row_shape, F32),
            pltpu.VMEM(row_shape, F32),
            pltpu.VMEM(row_shape, F32),
        ],
        compiler_params=params(32),
        name="observe",
    )(
        last,
        increment,
        forcing,
        lat_courant,
        lon_courant,
        error_weight,
        following,
        above,
        site_index,
        site_count.reshape(subs, NSTEP),
        site_value,
        site_weight,
    )
    below = shifted(edge, "space", -1)
    previous = shifted(end[-1], "tm", 1)

    lower = pl.pallas_call(
        lower_kernel,
        in_specs=[WHOLE] * 3,
        out_specs=WHOLE,
        out_shape=jax.ShapeDtypeStruct((subs * NSTEP, levels, 8, longs), F32),
        compiler_params=params(24),
        cost_estimate=pl.CostEstimate(
            flops=2 * 8 * 384 * 2048 * 256, bytes_accessed=2000000, transcendentals=0
        ),
        name="lower",
    )(cell, lane, dep)

    gradient, stats = pl.pallas_call(
        gradient_kernel,
        in_specs=[SCALAR] + [WHOLE] * 11 + [pl.BlockSpec(memory_space=pl.ANY)] * 2,
        out_specs=[WHOLE, WHOLE],
        out_shape=[
            jax.ShapeDtypeStruct(increment.shape, F32),
            jax.ShapeDtypeStruct((2, LANES), F32),
        ],
        scratch_shapes=[
            pltpu.VMEM((count, pairs, rows, longs), BF16),
            pltpu.VMEM((count, pairs, rows, longs), BF16),
            pltpu.VMEM((2 * pairs, 8, LANES), F32),
            pltpu.SemaphoreType.DMA((2, count)),
        ],
        compiler_params=params(32),
        name="gradient",
    )(
        last,
        increment,
        lat_courant,
        lon_courant,
        error_weight,
        following,
        end,
        previous,
        upper,
        lower,
        below,
        gram,
        pair_step,
        pair_change,
    )

    spread_out = jnp.broadcast_to(stats[None], (devices,) + stats.shape)
    stats = lax.all_to_all(spread_out, ("tm", "space"), 0, 0)

    field_spec = pl.BlockSpec(
        (1, some, rows, longs), lambda b: (b // (levels // some), b % (levels // some), 0, 0)
    )
    direction = pl.pallas_call(
        direction_kernel,
        grid=(blocks,),
        in_specs=[
            pl.BlockSpec(stats.shape, lambda b: (0, 0, 0)),
            field_spec,
            pair_spec,
            pair_spec,
        ],
        out_specs=field_spec,
        out_shape=jax.ShapeDtypeStruct(increment.shape, F32),
        scratch_shapes=[pltpu.VMEM((2 * pairs + 1, 8, LANES), F32)],
        compiler_params=params(16),
        name="direction",
    )(stats, gradient, pair_step, pair_change)
    return (gradient, direction)


def solution(mesh):
    return jax.shard_map(
        on_device,
        mesh=mesh,
        in_specs=(
            P("tm", None, "space", None),
            P("tm", None, "space", None),
            P(None, "space", None),
            P(None, "space", None),
            P(None, "space", None),
            P("tm", None, "space"),
            P("tm", None, "space"),
            P("tm", None, "space"),
            P("tm", None, "space"),
            P(None, "tm", None, "space", None),
            P(None, "tm", None, "space", None),
        ),
        out_specs=(P("tm", None, "space", None), P("tm", None, "space", None)),
        check_vma=False,
    )
```

```python
import functools

import jax
import jax.numpy as jnp
from jax import lax
from jax.experimental import pallas as pl
from jax.experimental.pallas import tpu as pltpu
from jax.sharding import PartitionSpec as P

NSTEP = 4
LANES = 128
F32 = jnp.float32
BF16 = jnp.bfloat16
WHOLE = pl.BlockSpec(memory_space=pltpu.VMEM)
SCALAR = pl.BlockSpec(memory_space=pltpu.SMEM)
FAR = pl.BlockSpec(memory_space=pl.ANY)


def shifted(shard, axis, by):
    count = lax.axis_size(axis)
    pairs = [(i, i + by) for i in range(count) if 0 <= i + by < count]
    return lax.ppermute(shard, axis, pairs)


def west(x):
    return jnp.concatenate([x[:, -1:], x[:, :-1]], axis=1)


def east(x):
    return jnp.concatenate([x[:, 1:], x[:, :1]], axis=1)


def rows_of(x):
    return lax.broadcasted_iota(jnp.int32, x.shape, 0)


def params(mib):
    return pltpu.CompilerParams(vmem_limit_bytes=mib << 20)


def halves(x):
    high = x.astype(BF16)
    return high, (x - high.astype(F32)).astype(BF16)


def edge_kernel(*refs):
    sources, (following_ref, edge_ref), homes, sems = refs[:6], refs[6:8], refs[8:14], refs[14]
    copies = [
        pltpu.make_async_copy(source, home, sems.at[i])
        for i, (source, home) in enumerate(zip(sources, homes))
    ]
    copies.append(pltpu.make_async_copy(sources[0].at[0], following_ref, sems.at[len(copies)]))
    for copy in copies:
        copy.start()
    for copy in copies[:4]:
        copy.wait()
    inc_ref, forcing_ref, lat_ref, lon_ref = homes[:4]
    levels = lat_ref.shape[0]

    def one(j, _):
        sub, lev = j // levels, j % levels
        x, push = inc_ref[sub, lev, 8:], forcing_ref[sub, lev, 8:]
        lat, lon = lat_ref[lev, 8:], lon_ref[lev, 8:]
        rest = 1.0 - lat - lon
        for step in range(NSTEP):
            edge_ref[j, step : step + 1, :] = x[7:8, :]
            if step < NSTEP - 1:
                x = rest * x + lat * pltpu.roll(x, 1, 0) + lon * west(x) + push
        return 0

    lax.fori_loop(0, edge_ref.shape[0], one, 0)
    for copy in copies[4:]:
        copy.wait()


def pairs_kernel(step_ref, change_ref, out_ref, acc_ref):
    pairs, subs, levels, rows, longs = step_ref.shape
    acc_ref[...] = jnp.zeros_like(acc_ref)

    def one(j, _):
        sub, lev = j // levels, j % levels
        steps = step_ref[:, sub, lev].reshape(pairs * rows, longs)
        changes = change_ref[:, sub, lev].reshape(pairs * rows, longs)
        left = jnp.concatenate([steps, changes], axis=0)
        acc_ref[...] += lax.dot_general(
            left, changes, (((1,), (1,)), ((), ())), preferred_element_type=F32
        )
        return 0

    lax.fori_loop(0, subs * levels, one, 0)
    total = acc_ref[...]
    row = lax.broadcasted_iota(jnp.int32, total.shape, 0)
    col = lax.broadcasted_iota(jnp.int32, total.shape, 1)
    total = jnp.where(row % rows == col % rows, total, 0.0)
    sums = [
        jnp.sum(total[v * rows : (v + 1) * rows], axis=0, keepdims=True) for v in range(2 * pairs)
    ]
    out_ref[...] = jnp.concatenate(sums, axis=0)


SPLIT = 8
INNER = 512
EDGE = 192
OUTER = 256


def one_hot(first, count, cell):
    place = lax.broadcasted_iota(jnp.int16, (count, cell.shape[1]), 0) + jnp.int16(first)
    return jnp.where(place == cell, jnp.ones((), BF16), jnp.zeros((), BF16))


def four_rows(ref, k, low, tile):
    lanes = slice(tile * LANES, (tile + 1) * LANES)
    return [ref[k, lev, low : low + 4, lanes] for lev in range(ref.shape[1])]


def look_up(blocks, first, cell, lane, store):
    table = jnp.concatenate(halves(jnp.concatenate([b.T for b in blocks], axis=1)), axis=0)
    chunk = 256
    for start in range(0, cell.shape[1], chunk):
        part = slice(start, start + chunk)
        hot = one_hot(first, table.shape[1], cell[:, part])
        got = jnp.dot(table, hot, preferred_element_type=F32)
        got = got[:LANES] + got[LANES:]
        mine = lax.broadcasted_iota(jnp.int32, (LANES, chunk), 0) == lane[:, part]
        store(part, jnp.sum(jnp.where(mine, got, 0.0), axis=0, keepdims=True))


def inner_kernel(
    inc_ref,
    forcing_ref,
    lat_ref,
    lon_ref,
    index_ref,
    step_far,
    change_far,
    rows_ref,
    end_ref,
    gram_ref,
    state_ref,
    acc_ref,
    seen_ref,
    cell_ref,
    lane_ref,
    step_ref,
    change_ref,
    sems,
):
    subs, levels, rows, longs = inc_ref.shape
    copies = [
        pltpu.make_async_copy(step_far, step_ref, sems.at[0]),
        pltpu.make_async_copy(change_far, change_ref, sems.at[1]),
    ]
    for copy in copies:
        copy.start()
    tiles = -(-longs // LANES)
    state_ref[:, :, :, longs - longs % LANES :] = jnp.zeros(
        (subs * NSTEP, levels, rows, LANES), F32
    )
    for sub in range(subs):
        index = index_ref[sub]
        row = ((index.astype(F32) + 0.5) * (1.0 / longs)).astype(jnp.int32)
        lon = index - row * longs
        lev, lat = row // rows, row % rows
        tile, lane = lon // LANES, lon % LANES
        band = tile * 16 + lev * 4 + lat % 4
        cell = jnp.where(
            lat >= 8,
            tile * 32 + lev * 8 + lat - 8,
            jnp.where(
                lat < 4,
                INNER + band,
                jnp.where(tile < SPLIT, 384 + band, INNER + EDGE - SPLIT * 16 + band),
            ),
        )
        for step in range(NSTEP):
            k = sub * NSTEP + step
            cell_ref[k] = cell[step : step + 1]
            lane_ref[k] = lane[step : step + 1]
            rows_ref[1, k : k + 1, :] = cell[step : step + 1].astype(F32)
            rows_ref[2, k : k + 1, :] = lane[step : step + 1].astype(F32)

    def tangent(sub, lev):
        x = inc_ref[sub, lev]
        lat, lon, push = lat_ref[lev], lon_ref[lev], forcing_ref[sub, lev]
        rest = 1.0 - lat - lon
        for step in range(NSTEP):
            x = rest * x + lat * pltpu.roll(x, 1, 0) + lon * west(x) + push
            state_ref[sub * NSTEP + step, lev, :, :longs] = x
        end_ref[sub, lev] = x[8:]

    def gather(k):
        blocks = []
        for first in range(0, tiles, 4):
            part = [
                state_ref[k, :, 8:, t * LANES : (t + 1) * LANES].reshape(levels * 8, LANES)
                for t in range(first, first + 4)
            ]
            blocks.append(jnp.concatenate(part, axis=0))
        part = []
        for t in range(SPLIT):
            part += four_rows(state_ref, k, 4, t)
        blocks.append(jnp.concatenate(part, axis=0))

        def store(part, value):
            seen_ref[k, :, part] = value

        look_up(blocks, 0, cell_ref[k].astype(jnp.int16), lane_ref[k], store)

    def first(lev, _):
        tangent(0, lev)
        return 0

    lax.fori_loop(0, levels, first, 0)
    for sub in range(subs):

        def both(i, _, sub=sub):
            gather(sub * NSTEP + i)
            if sub + 1 < subs:
                tangent(sub + 1, i)
            return 0

        lax.fori_loop(0, NSTEP, both, 0, unroll=2)
    for k in range(subs * NSTEP):
        rows_ref[0, k : k + 1, :] = seen_ref[k]
    for copy in copies:
        copy.wait()
    pairs_kernel(step_ref, change_ref, gram_ref, acc_ref)


def outer_kernel(
    last_ref,
    inc_ref,
    forcing_ref,
    lat_ref,
    lon_ref,
    ew_ref,
    next_ref,
    above_ref,
    count_ref,
    value_far,
    weight_far,
    rows_ref,
    upper_ref,
    end_ref,
    sent_ref,
    edge_ref,
    inject_ref,
    dep_ref,
    state_ref,
    value_ref,
    weight_ref,
    seen_ref,
    cell_ref,
    lane_ref,
    dep_row,
    sems,
):
    subs, levels, _, longs = inc_ref.shape
    slots = value_ref.shape[2]
    tiles = -(-longs // LANES)
    copies = [
        pltpu.make_async_copy(value_far, value_ref, sems.at[0]),
        pltpu.make_async_copy(weight_far, weight_ref, sems.at[1]),
    ]
    for copy in copies:
        copy.start()
    state_ref[:, :, :, longs - longs % LANES :] = jnp.zeros((subs * NSTEP, levels, 8, LANES), F32)
    take_rows(rows_ref, cell_ref, lane_ref)

    def tangent(j, _):
        sub, lev = j // levels, j % levels
        x, push = inc_ref[sub, lev, :8], forcing_ref[sub, lev, :8]
        lat, lon = lat_ref[lev, :8], lon_ref[lev, :8]
        rest = 1.0 - lat - lon
        top = rows_of(x) == 0
        for step in range(NSTEP):
            above = jnp.where(top, above_ref[j, step : step + 1, :], pltpu.roll(x, 1, 0))
            x = rest * x + lat * above + lon * west(x) + push
            state_ref[sub * NSTEP + step, lev, :, :longs] = x
        end_ref[sub, lev] = x
        return 0

    lax.fori_loop(0, subs * levels, tangent, 0)
    sent_ref[:, :8] = end_ref[subs - 1]
    sent_ref[:, 8:] = upper_ref[subs - 1]

    def gather(k, _):
        part = []
        for t in range(tiles):
            part += four_rows(state_ref, k, 0, t)
        for t in range(SPLIT, tiles):
            part += four_rows(state_ref, k, 4, t)
        half = len(part) // 2
        blocks = [jnp.concatenate(part[:half], axis=0), jnp.concatenate(part[half:], axis=0)]

        def store(part, value):
            seen_ref[k, :, part] = value

        look_up(blocks, INNER, cell_ref[k].astype(jnp.int16), lane_ref[k], store)
        return 0

    lax.fori_loop(0, subs * NSTEP, gather, 0, unroll=2)

    slot = lax.broadcasted_iota(jnp.int32, (NSTEP, slots), 1)
    row = lax.broadcasted_iota(jnp.int32, (NSTEP, slots), 0)
    for copy in copies:
        copy.wait()
    for sub in range(subs):
        ks = range(sub * NSTEP, (sub + 1) * NSTEP)
        seen = rows_ref[0, ks.start : ks.stop, :]
        seen = seen + jnp.concatenate([seen_ref[k] for k in ks], axis=0)
        live = slot < 0
        for step in range(NSTEP):
            live = live | ((row == step) & (slot < count_ref[sub, step]))
        dep = jnp.where(live, weight_ref[sub] * (value_ref[sub] - seen), 0.0)
        dep_ref[ks.start : ks.stop, :] = dep
        for step in range(NSTEP):
            dep_row[ks[step]] = dep[step : step + 1]

    def scatter(k, _):
        cell = cell_ref[k].astype(jnp.int16)
        out = spread(one_hot(INNER, EDGE, cell), lane_ref[k], dep_row[k])
        store_four(inject_ref, k, 0, out, 0, tiles)
        return 0

    lax.fori_loop(0, subs * NSTEP, scatter, 0, unroll=2)

    for sub in range(subs):
        for lev in range(levels):
            j = sub * levels + lev
            later = next_ref[lev, :8] if sub == subs - 1 else inc_ref[sub + 1, lev, :8]
            d = ew_ref[lev, :8] * (later - end_ref[sub, lev])
            if sub == subs - 1:
                d = d * last_ref[0]
            lat, lon = lat_ref[lev, :8], lon_ref[lev, :8]
            rest = 1.0 - lat - lon
            for step in range(NSTEP - 1, -1, -1):
                d = d + inject_ref[sub * NSTEP + step, lev]
                part = lat * d
                edge_ref[j, step : step + 1, :] = part[:1, :]
                if step:
                    d = rest * d + pltpu.roll(part, 7, 0) + east(lon * d)


def spread(hot, lane, dep):
    high, low = halves(dep)
    mine = lax.broadcasted_iota(jnp.int16, (LANES, dep.shape[1]), 0) == lane.astype(jnp.int16)
    zero = jnp.zeros((), BF16)
    values = jnp.concatenate([jnp.where(mine, high, zero), jnp.where(mine, low, zero)], axis=0)
    out = lax.dot_general(hot, values, (((1,), (1,)), ((), ())), preferred_element_type=F32)
    return out[:, :LANES] + out[:, LANES:]


def take_rows(rows_ref, cell_ref, lane_ref):
    for k in range(rows_ref.shape[1]):
        cell_ref[k] = rows_ref[1, k : k + 1, :].astype(jnp.int32)
        lane_ref[k] = rows_ref[2, k : k + 1, :].astype(jnp.int32)


def store_tile(ref, k, lev, low, tile, x):
    longs = ref.shape[3]
    stop = min((tile + 1) * LANES, longs)
    ref[k, lev, low : low + x.shape[0], tile * LANES : stop] = x[:, : stop - tile * LANES]


def store_four(ref, k, low, out, first, stop):
    levels = ref.shape[1]
    for t in range(first, stop):
        for lev in range(levels):
            at = ((t - first) * levels + lev) * 4
            store_tile(ref, k, lev, low, t, out[at : at + 4])


def scatter_kernel(
    rows_ref, dep_ref, part_ref, lower_ref, upper_ref, cell_ref, lane_ref, dep_row
):
    count, levels, _, longs = lower_ref.shape
    take_rows(rows_ref, cell_ref, lane_ref)
    for k in range(count):
        dep_row[k] = dep_ref[k : k + 1, :]
    tiles = -(-longs // LANES)
    high = tiles * levels * 8

    def one(k, _):
        cell = cell_ref[k].astype(jnp.int16)
        hot = jnp.concatenate(
            [one_hot(0, INNER, cell), one_hot(INNER + EDGE, OUTER - EDGE, cell)], axis=0
        )
        out = spread(hot, lane_ref[k], dep_row[k])
        for t in range(tiles):
            for lev in range(levels):
                at = (t * levels + lev) * 8
                store_tile(upper_ref, k, lev, 0, t, out[at : at + 8])
        lower_ref[k, :, :4] = part_ref[k, :, :4]
        store_four(lower_ref, k, 4, out[high:], 0, tiles)
        return 0

    lax.fori_loop(0, count, one, 0, unroll=2)


def gradient_kernel(
    last_ref,
    inc_ref,
    lat_ref,
    lon_ref,
    ew_ref,
    next_ref,
    end_low_ref,
    end_high_ref,
    previous_ref,
    lower_ref,
    upper_ref,
    below_ref,
    gram_ref,
    step_ref,
    change_ref,
    grad_ref,
    stats_ref,
    dots_ref,
):
    subs, levels, rows, longs = inc_ref.shape
    pairs = step_ref.shape[0]
    count = subs * levels
    dots_ref[...] = jnp.zeros_like(dots_ref)

    def one(j, _):
        sub, lev = j // levels, j % levels
        ew = ew_ref[lev]
        final = sub == subs - 1
        later = jnp.where(final, next_ref[lev], inc_ref[jnp.minimum(sub + 1, subs - 1), lev])
        d = ew * (later - jnp.concatenate([end_low_ref[sub, lev], end_high_ref[sub, lev]], axis=0))
        d = d * jnp.where(final, last_ref[0], 1.0)
        lat, lon = lat_ref[lev], lon_ref[lev]
        rest = 1.0 - lat - lon
        bottom = rows_of(d) == rows - 1
        for step in range(NSTEP - 1, -1, -1):
            k = sub * NSTEP + step
            d = d + jnp.concatenate([lower_ref[k, lev], upper_ref[k, lev]], axis=0)
            part = lat * d
            below = jnp.where(
                bottom, below_ref[j, step : step + 1, :], pltpu.roll(part, rows - 1, 0)
            )
            d = rest * d + below + east(lon * d)
        before = jnp.maximum(sub - 1, 0)
        before = jnp.concatenate([end_low_ref[before, lev], end_high_ref[before, lev]], axis=0)
        earlier = jnp.where(sub == 0, previous_ref[lev], before)
        g = ew * (inc_ref[sub, lev] - earlier) - d
        grad_ref[sub, lev] = g
        for i in range(pairs):
            for which, ref in enumerate((step_ref, change_ref)):
                dots_ref[which * pairs + i] += fold(g * ref[i, sub, lev].astype(F32))
        return 0

    lax.fori_loop(0, count, one, 0)
    sums = [jnp.sum(dots_ref[v], axis=0, keepdims=True) for v in range(2 * pairs)]
    sums = jnp.concatenate(sums, axis=0)
    dots = jnp.sum(sums, axis=1, keepdims=True)
    raw = gram_ref[...]
    row = lax.broadcasted_iota(jnp.int32, raw.shape, 0)
    col = lax.broadcasted_iota(jnp.int32, raw.shape, 1)
    group = col // rows
    here = col % rows == row
    out = jnp.zeros((1, raw.shape[1]), F32)
    for c in range(pairs):
        part = jnp.sum(jnp.where(group == c, raw, 0.0), axis=1, keepdims=True)
        out += jnp.sum(jnp.where(here & (group == c), part, 0.0), axis=0, keepdims=True)
    stats_ref[0:1, :] = out
    stats_ref[1:2, :] = jnp.sum(jnp.where(here, dots, 0.0), axis=0, keepdims=True)


def fold(x):
    longs = x.shape[1]
    whole = longs - longs % LANES
    x = x[:8] + x[8:]
    out = x[:, :LANES]
    for first in range(LANES, whole, LANES):
        out = out + x[:, first : first + LANES]
    if whole < longs:
        tail = jnp.concatenate(
            [x[:, whole:], jnp.zeros((8, LANES - (longs - whole)), F32)], axis=1
        )
        out = out + tail
    return out


def direction_kernel(
    stats_ref, grad_ref, step_ref, change_ref, grad_out, direction_out, coef_ref, out_ref, sems
):
    pairs, subs, levels, _, _ = step_ref.shape
    both = 2 * pairs
    count = subs * levels
    handed = pltpu.make_async_copy(grad_ref, grad_out, sems.at[count])
    handed.start()
    gram = jnp.sum(stats_ref[:, 0, :], axis=0, keepdims=True)
    dots = jnp.sum(stats_ref[:, 1, :], axis=0, keepdims=True)
    shape = (both, LANES)
    row = lax.broadcasted_iota(jnp.int32, shape, 0)
    col = lax.broadcasted_iota(jnp.int32, shape, 1)
    group, inner = col // both, col % both
    gram = jnp.broadcast_to(gram, shape)
    dots = jnp.broadcast_to(dots, shape)

    def column(mask, x):
        return jnp.sum(jnp.where(mask, x, 0.0), axis=1, keepdims=True)

    dots = column((inner == row) & (group == 0), dots)
    by_change = [column((inner == row) & (group == c), gram) for c in range(pairs)]
    by_step = [column((group == row) & (inner == i), gram)[:pairs] for i in range(pairs)]
    diagonal = column((group == row) & (inner == row), gram)[:pairs]
    rho = 1.0 / diagonal
    with_step, with_change = dots[:pairs], dots[pairs:]
    alphas = [None] * pairs
    for i in range(pairs - 1, -1, -1):
        alphas[i] = rho[i : i + 1] * with_step[i : i + 1]
        with_step = with_step - alphas[i] * by_change[i][:pairs]
        with_change = with_change - alphas[i] * by_change[i][pairs:]
    gamma = diagonal[pairs - 1 : pairs] / by_change[pairs - 1][both - 1 : both]
    with_change = gamma * with_change
    coef_ref[both] = jnp.broadcast_to(gamma, (8, LANES))
    for i in range(pairs):
        beta = rho[i : i + 1] * with_change[i : i + 1]
        rise = alphas[i] - beta
        with_change = with_change + rise * by_step[i]
        coef_ref[i] = jnp.broadcast_to(rise, (8, LANES))
        coef_ref[pairs + i] = jnp.broadcast_to(-gamma * alphas[i], (8, LANES))


    def copy(j):
        sub, lev = j // levels, j % levels
        return pltpu.make_async_copy(
            out_ref.at[sub, lev], direction_out.at[sub, lev], sems.at[j]
        )

    def one(j, _):
        sub, lev = j // levels, j % levels
        total = coef_ref[both][:1, :1] * grad_ref[sub, lev]
        for i in range(pairs):
            total += coef_ref[i][:1, :1] * step_ref[i, sub, lev].astype(F32)
            total += coef_ref[pairs + i][:1, :1] * change_ref[i, sub, lev].astype(F32)
        out_ref[sub, lev] = total
        copy(j).start()
        return 0

    lax.fori_loop(0, count, one, 0)
    for j in range(count):
        copy(j).wait()
    handed.wait()


def on_device(
    increment,
    forcing,
    lat_courant,
    lon_courant,
    error_weight,
    site_index,
    site_count,
    site_value,
    site_weight,
    pair_step,
    pair_change,
):
    subs, levels, rows, longs = increment.shape
    pairs = pair_step.shape[0]
    slots = site_index.shape[2]
    count = subs * levels
    wide = -(-longs // LANES) * LANES
    devices = lax.axis_size("tm") * lax.axis_size("space")
    last = jnp.where(lax.axis_index("tm") == lax.axis_size("tm") - 1, 0.0, 1.0)
    last = last.astype(F32).reshape(1)

    def like(x):
        return pltpu.VMEM(x.shape, x.dtype)

    def floats(*shape):
        return pltpu.VMEM(shape, F32)

    def cost(flops):
        return pl.CostEstimate(flops=flops, bytes_accessed=1 << 20, transcendentals=0)

    def far(*arrays):
        return [pltpu.with_memory_space_constraint(x, pltpu.HBM) for x in arrays]

    arguments = (increment, forcing, lat_courant, lon_courant, error_weight, site_index)
    following, edge, inc, push, lat, lon, ew, index = pl.pallas_call(
        edge_kernel,
        in_specs=[FAR] * len(arguments),
        out_specs=[WHOLE] * (2 + len(arguments)),
        out_shape=[floats(levels, rows, longs), floats(count, NSTEP, longs)]
        + [like(x) for x in arguments],
        scratch_shapes=[pltpu.SemaphoreType.DMA((len(arguments) + 1,))],
        compiler_params=params(16),
        name="edge",
    )(*far(*arguments))
    above = shifted(edge, "space", 1)
    following = shifted(following, "tm", -1)

    row_shape = (subs * NSTEP, 1, slots)
    row_scratch = [
        pltpu.VMEM(row_shape, F32),
        pltpu.VMEM(row_shape, jnp.int32),
        pltpu.VMEM(row_shape, jnp.int32),
    ]
    rows_of_slots, end_high, gram = pl.pallas_call(
        inner_kernel,
        in_specs=[WHOLE] * 5 + [FAR] * 2,
        out_specs=[WHOLE] * 3,
        out_shape=[
            floats(3, subs * NSTEP, slots),
            floats(subs, levels, 8, longs),
            floats(2 * pairs, pairs * rows),
        ],
        scratch_shapes=[
            pltpu.VMEM((subs * NSTEP, levels, rows, wide), F32),
            pltpu.VMEM((2 * pairs * rows, pairs * rows), F32),
        ]
        + row_scratch
        + [
            pltpu.VMEM(pair_step.shape, BF16),
            pltpu.VMEM(pair_step.shape, BF16),
            pltpu.SemaphoreType.DMA((2,)),
        ],
        compiler_params=params(28),
        cost_estimate=cost(8 * 10**9),
        name="inner",
    )(inc, push, lat, lon, index, *far(pair_step, pair_change))

    end_low, sent, edge, part, dep = pl.pallas_call(
        outer_kernel,
        in_specs=[SCALAR] + [WHOLE] * 7 + [SCALAR] + [FAR] * 2 + [WHOLE] * 2,
        out_specs=[WHOLE] * 5,
        out_shape=[
            floats(subs, levels, 8, longs),
            floats(levels, rows, longs),
            floats(count, NSTEP, longs),
            floats(subs * NSTEP, levels, 8, longs),
            floats(subs * NSTEP, slots),
        ],
        scratch_shapes=[
            pltpu.VMEM((subs * NSTEP, levels, 8, wide), F32),
            pltpu.VMEM(site_value.shape, F32),
            pltpu.VMEM(site_value.shape, F32),
        ]
        + row_scratch
        + [pltpu.VMEM(row_shape, F32), pltpu.SemaphoreType.DMA((2,))],
        compiler_params=params(24),
        cost_estimate=cost(5 * 10**9),
        name="outer",
    )(
        last,
        inc,
        push,
        lat,
        lon,
        ew,
        following,
        above,
        site_count.reshape(subs, NSTEP),
        *far(site_value, site_weight),
        rows_of_slots,
        end_high,
    )
    below = shifted(edge, "space", -1)
    previous = shifted(sent, "tm", 1)

    lower, upper = pl.pallas_call(
        scatter_kernel,
        in_specs=[WHOLE] * 3,
        out_specs=[WHOLE] * 2,
        out_shape=[floats(subs * NSTEP, levels, 8, longs)] * 2,
        scratch_shapes=row_scratch[1:] + row_scratch[:1],
        compiler_params=params(24),
        cost_estimate=cost(6 * 10**9),
        name="scatter",
    )(rows_of_slots, dep, part)

    gradient, stats = pl.pallas_call(
        gradient_kernel,
        in_specs=[SCALAR] + [WHOLE] * 14,
        out_specs=[WHOLE] * 2,
        out_shape=[like(increment), floats(2, LANES)],
        scratch_shapes=[pltpu.VMEM((2 * pairs, 8, LANES), F32)],
        compiler_params=params(16),
        name="gradient",
    )(
        last,
        inc,
        lat,
        lon,
        ew,
        following,
        end_low,
        end_high,
        previous,
        lower,
        upper,
        below,
        gram,
        pair_step,
        pair_change,
    )

    stats = jnp.broadcast_to(stats[None], (devices,) + stats.shape)
    stats = lax.all_to_all(stats, ("tm", "space"), 0, 0)

    return pl.pallas_call(
        direction_kernel,
        in_specs=[WHOLE] * 4,
        out_specs=[FAR] * 2,
        out_shape=[jax.ShapeDtypeStruct(increment.shape, F32)] * 2,
        scratch_shapes=[
            pltpu.VMEM((2 * pairs + 1, 8, LANES), F32),
            pltpu.VMEM(increment.shape, F32),
            pltpu.SemaphoreType.DMA((count + 1,)),
        ],
        compiler_params=params(16),
        name="direction",
    )(stats, gradient, pair_step, pair_change)


def solution(mesh):
    return jax.shard_map(
        on_device,
        mesh=mesh,
        in_specs=(
            P("tm", None, "space", None),
            P("tm", None, "space", None),
            P(None, "space", None),
            P(None, "space", None),
            P(None, "space", None),
            P("tm", None, "space"),
            P("tm", None, "space"),
            P("tm", None, "space"),
            P("tm", None, "space"),
            P(None, "tm", None, "space", None),
            P(None, "tm", None, "space", None),
        ),
        out_specs=(P("tm", None, "space", None), P("tm", None, "space", None)),
        check_vma=False,
    )
```

```python
import functools

import jax
import jax.numpy as jnp
from jax import lax
from jax.experimental import pallas as pl
from jax.experimental.pallas import tpu as pltpu
from jax.sharding import PartitionSpec as P

NSTEP = 4
LANES = 128
F32 = jnp.float32
BF16 = jnp.bfloat16
WHOLE = pl.BlockSpec(memory_space=pltpu.VMEM)
SCALAR = pl.BlockSpec(memory_space=pltpu.SMEM)
FAR = pl.BlockSpec(memory_space=pl.ANY)


def shifted(shard, axis, by):
    count = lax.axis_size(axis)
    pairs = [(i, i + by) for i in range(count) if 0 <= i + by < count]
    return lax.ppermute(shard, axis, pairs)


def west(x):
    return jnp.concatenate([x[:, -1:], x[:, :-1]], axis=1)


def east(x):
    return jnp.concatenate([x[:, 1:], x[:, :1]], axis=1)


def rows_of(x):
    return lax.broadcasted_iota(jnp.int32, x.shape, 0)


def params(mib):
    return pltpu.CompilerParams(vmem_limit_bytes=mib << 20)


def halves(x):
    high = x.astype(BF16)
    return high, (x - high.astype(F32)).astype(BF16)


def edge_kernel(*refs):
    sources, (following_ref, edge_ref), homes, sems = refs[:6], refs[6:8], refs[8:14], refs[14]
    def lower(ref):
        return ref.at[:, :, 8:] if len(ref.shape) == 4 else ref.at[:, 8:]

    def upper(ref):
        return ref.at[:, :, :8] if len(ref.shape) == 4 else ref.at[:, :8]

    pieces = [(lower(source), lower(home)) for source, home in zip(sources[:4], homes[:4])]
    pieces += [(upper(source), upper(home)) for source, home in zip(sources[:4], homes[:4])]
    pieces += list(zip(sources[4:], homes[4:])) + [(sources[0].at[0], following_ref)]
    copies = [
        pltpu.make_async_copy(source, home, sems.at[i]) for i, (source, home) in enumerate(pieces)
    ]
    for copy in copies:
        copy.start()
    for copy in copies[:4]:
        copy.wait()
    inc_ref, forcing_ref, lat_ref, lon_ref = homes[:4]
    levels = lat_ref.shape[0]

    def one(j, _):
        sub, lev = j // levels, j % levels
        x, push = inc_ref[sub, lev, 8:], forcing_ref[sub, lev, 8:]
        lat, lon = lat_ref[lev, 8:], lon_ref[lev, 8:]
        rest = 1.0 - lat - lon
        for step in range(NSTEP):
            edge_ref[j, step : step + 1, :] = x[7:8, :]
            if step < NSTEP - 1:
                x = rest * x + lat * pltpu.roll(x, 1, 0) + lon * west(x) + push
        return 0

    lax.fori_loop(0, edge_ref.shape[0], one, 0, unroll=4)
    for copy in copies[4:]:
        copy.wait()


def pair_products(step_ref, change_ref, acc_ref, j):
    pairs, _, levels, rows, longs = step_ref.shape
    sub, lev = j // levels, j % levels
    steps = step_ref[:, sub, lev].reshape(pairs * rows, longs)
    changes = change_ref[:, sub, lev].reshape(pairs * rows, longs)
    both = jnp.concatenate([steps, changes], axis=0)
    acc_ref[...] += lax.dot_general(
        changes, both, (((1,), (1,)), ((), ())), preferred_element_type=F32
    )


def pair_sums(acc_ref, rows, out_ref):
    total = acc_ref[...].T
    row = lax.broadcasted_iota(jnp.int32, total.shape, 0)
    col = lax.broadcasted_iota(jnp.int32, total.shape, 1)
    total = jnp.where(row % rows == col % rows, total, 0.0)
    sums = [
        jnp.sum(total[first : first + rows], axis=0, keepdims=True)
        for first in range(0, total.shape[0], rows)
    ]
    sums = jnp.concatenate(sums, axis=0)
    row, group, inner = lane_places(sums.shape)
    out = jnp.zeros(sums.shape, F32)
    for c in range(sums.shape[1] // rows):
        part = jnp.sum(jnp.where(group == c, sums, 0.0), axis=1, keepdims=True)
        out = jnp.where((group == c) & (inner == row), part, out)
    out_ref[...] = out


def lane_places(shape):
    row = lax.broadcasted_iota(jnp.int32, shape, 0)
    col = lax.broadcasted_iota(jnp.int32, shape, 1)
    return row, col // shape[0], col % shape[0]


WITH_CHANGE = 5
WITH_STEP = 6


SPLIT = 8
INNER = 512
EDGE = 192
OUTER = 256


def one_hot(first, count, cell):
    place = lax.broadcasted_iota(jnp.int16, (count, cell.shape[1]), 0) + jnp.int16(first)
    return jnp.where(place == cell, jnp.ones((), BF16), jnp.zeros((), BF16))


def four_rows(ref, k, low, tile):
    lanes = slice(tile * LANES, (tile + 1) * LANES)
    return [ref[k, lev, low : low + 4, lanes] for lev in range(ref.shape[1])]


def look_up(blocks, first, cell, lane, store):
    table = jnp.concatenate(halves(jnp.concatenate([b.T for b in blocks], axis=1)), axis=0)
    chunk = 256
    for start in range(0, cell.shape[1], chunk):
        part = slice(start, start + chunk)
        hot = one_hot(first, table.shape[1], cell[:, part])
        got = jnp.dot(table, hot, preferred_element_type=F32)
        got = got[:LANES] + got[LANES:]
        mine = lax.broadcasted_iota(jnp.int32, (LANES, chunk), 0) == lane[:, part]
        store(part, jnp.sum(jnp.where(mine, got, 0.0), axis=0, keepdims=True))


def inner_kernel(
    inc_ref,
    forcing_ref,
    lat_ref,
    lon_ref,
    index_ref,
    step_far,
    change_far,
    rows_ref,
    end_ref,
    gram_ref,
    step_ref,
    change_ref,
    state_ref,
    acc_ref,
    seen_ref,
    cell_ref,
    lane_ref,
    sems,
):
    subs, levels, rows, longs = inc_ref.shape
    copies = [
        pltpu.make_async_copy(far.at[i], near.at[i], sems.at[which, i])
        for i in range(step_ref.shape[0])
        for which, (far, near) in enumerate(((step_far, step_ref), (change_far, change_ref)))
    ]
    for copy in copies:
        copy.start()
    tiles = -(-longs // LANES)
    state_ref[:, :, :, longs - longs % LANES :] = jnp.zeros(
        (subs * NSTEP, levels, rows, LANES), F32
    )
    for sub in range(subs):
        index = index_ref[sub]
        row = ((index.astype(F32) + 0.5) * (1.0 / longs)).astype(jnp.int32)
        lon = index - row * longs
        lev, lat = row // rows, row % rows
        tile, lane = lon // LANES, lon % LANES
        band = tile * 16 + lev * 4 + lat % 4
        cell = jnp.where(
            lat >= 8,
            tile * 32 + lev * 8 + lat - 8,
            jnp.where(
                lat < 4,
                INNER + band,
                jnp.where(tile < SPLIT, 384 + band, INNER + EDGE - SPLIT * 16 + band),
            ),
        )
        for step in range(NSTEP):
            k = sub * NSTEP + step
            cell_ref[k] = cell[step : step + 1]
            lane_ref[k] = lane[step : step + 1]
            rows_ref[1, k : k + 1, :] = cell[step : step + 1].astype(F32)
            rows_ref[2, k : k + 1, :] = lane[step : step + 1].astype(F32)

    def tangent(sub, lev):
        x = inc_ref[sub, lev]
        lat, lon, push = lat_ref[lev], lon_ref[lev], forcing_ref[sub, lev]
        rest = 1.0 - lat - lon
        for step in range(NSTEP):
            x = rest * x + lat * pltpu.roll(x, 1, 0) + lon * west(x) + push
            state_ref[sub * NSTEP + step, lev, :, :longs] = x
        end_ref[sub, lev] = x[8:]

    def gather(k):
        blocks = []
        for first in range(0, tiles, 4):
            part = [
                state_ref[k, :, 8:, t * LANES : (t + 1) * LANES].reshape(levels * 8, LANES)
                for t in range(first, first + 4)
            ]
            blocks.append(jnp.concatenate(part, axis=0))
        part = []
        for t in range(SPLIT):
            part += four_rows(state_ref, k, 4, t)
        blocks.append(jnp.concatenate(part, axis=0))

        def store(part, value):
            seen_ref[k, :, part] = value

        look_up(blocks, 0, cell_ref[k].astype(jnp.int16), lane_ref[k], store)

    def first(lev, _):
        tangent(0, lev)
        return 0

    lax.fori_loop(0, levels, first, 0, unroll=2)
    acc_ref[...] = jnp.zeros_like(acc_ref)

    count = subs * levels
    for i in range(NSTEP // 2):
        gather(i)
        tangent(1, 2 * i)
        tangent(1, 2 * i + 1)
    for copy in copies:
        copy.wait()
    for i in range(NSTEP // 2):
        gather(NSTEP // 2 + i)
        pair_products(step_ref, change_ref, acc_ref, 2 * i)
        pair_products(step_ref, change_ref, acc_ref, 2 * i + 1)
    for i in range(NSTEP):
        gather(NSTEP + i)
        pair_products(step_ref, change_ref, acc_ref, count // 2 + i)
    for k in range(subs * NSTEP):
        rows_ref[0, k : k + 1, :] = seen_ref[k]
    pair_sums(acc_ref, rows, gram_ref)


def outer_kernel(
    last_ref,
    inc_ref,
    forcing_ref,
    lat_ref,
    lon_ref,
    ew_ref,
    next_ref,
    above_ref,
    count_ref,
    value_far,
    weight_far,
    rows_ref,
    upper_ref,
    end_ref,
    sent_ref,
    edge_ref,
    inject_ref,
    dep_ref,
    state_ref,
    value_ref,
    weight_ref,
    seen_ref,
    cell_ref,
    lane_ref,
    dep_row,
    sems,
):
    subs, levels, _, longs = inc_ref.shape
    slots = value_ref.shape[2]
    tiles = -(-longs // LANES)
    copies = [
        pltpu.make_async_copy(value_far, value_ref, sems.at[0]),
        pltpu.make_async_copy(weight_far, weight_ref, sems.at[1]),
    ]
    for copy in copies:
        copy.start()
    state_ref[:, :, :, longs - longs % LANES :] = jnp.zeros((subs * NSTEP, levels, 8, LANES), F32)
    take_rows(rows_ref, cell_ref, lane_ref)

    def tangent(sub, lev):
        j = sub * levels + lev
        x, push = inc_ref[sub, lev, :8], forcing_ref[sub, lev, :8]
        lat, lon = lat_ref[lev, :8], lon_ref[lev, :8]
        rest = 1.0 - lat - lon
        top = rows_of(x) == 0
        for step in range(NSTEP):
            above = jnp.where(top, above_ref[j, step : step + 1, :], pltpu.roll(x, 1, 0))
            x = rest * x + lat * above + lon * west(x) + push
            state_ref[sub * NSTEP + step, lev, :, :longs] = x
        end_ref[sub, lev] = x
        if sub == subs - 1:
            sent_ref[lev, :8] = x
            sent_ref[lev, 8:] = upper_ref[sub, lev]

    def gather(k):
        part = []
        for t in range(tiles):
            part += four_rows(state_ref, k, 0, t)
        for t in range(SPLIT, tiles):
            part += four_rows(state_ref, k, 4, t)
        half = len(part) // 2
        blocks = [jnp.concatenate(part[:half], axis=0), jnp.concatenate(part[half:], axis=0)]

        def store(part, value):
            seen_ref[k, :, part] = value

        look_up(blocks, INNER, cell_ref[k].astype(jnp.int16), lane_ref[k], store)

    slot = lax.broadcasted_iota(jnp.int32, (NSTEP, slots), 1)
    row = lax.broadcasted_iota(jnp.int32, (NSTEP, slots), 0)

    def departures(sub):
        ks = range(sub * NSTEP, (sub + 1) * NSTEP)
        seen = rows_ref[0, ks.start : ks.stop, :]
        seen = seen + jnp.concatenate([seen_ref[k] for k in ks], axis=0)
        live = slot < 0
        for step in range(NSTEP):
            live = live | ((row == step) & (slot < count_ref[sub, step]))
        dep = jnp.where(live, weight_ref[sub] * (value_ref[sub] - seen), 0.0)
        dep_ref[ks.start : ks.stop, :] = dep
        for step in range(NSTEP):
            dep_row[ks[step]] = dep[step : step + 1]

    def scatter(k):
        cell = cell_ref[k].astype(jnp.int16)
        out = spread(one_hot(INNER, EDGE, cell), lane_ref[k], dep_row[k])
        store_four(inject_ref, k, 0, out, 0, tiles)

    def dual_edge(sub, lev):
        j = sub * levels + lev
        later = next_ref[lev, :8] if sub == subs - 1 else inc_ref[sub + 1, lev, :8]
        d = ew_ref[lev, :8] * (later - end_ref[sub, lev])
        if sub == subs - 1:
            d = d * last_ref[0]
        lat, lon = lat_ref[lev, :8], lon_ref[lev, :8]
        rest = 1.0 - lat - lon
        for step in range(NSTEP - 1, -1, -1):
            d = d + inject_ref[sub * NSTEP + step, lev]
            part = lat * d
            edge_ref[j, step : step + 1, :] = part[:1, :]
            if step:
                d = rest * d + pltpu.roll(part, 7, 0) + east(lon * d)

    for lev in range(levels):
        tangent(0, lev)
    for i in range(NSTEP):
        gather(i)
        tangent(1, i)
    for copy in copies:
        copy.wait()
    departures(0)
    for i in range(NSTEP):
        gather(NSTEP + i)
        scatter(i)
    departures(1)
    for i in range(NSTEP):
        scatter(NSTEP + i)
        dual_edge(0, i)
    for lev in range(levels):
        dual_edge(1, lev)


def spread(hot, lane, dep):
    high, low = halves(dep)
    mine = lax.broadcasted_iota(jnp.int16, (LANES, dep.shape[1]), 0) == lane.astype(jnp.int16)
    zero = jnp.zeros((), BF16)
    values = jnp.concatenate([jnp.where(mine, high, zero), jnp.where(mine, low, zero)], axis=0)
    out = lax.dot_general(hot, values, (((1,), (1,)), ((), ())), preferred_element_type=F32)
    return out[:, :LANES] + out[:, LANES:]


def take_rows(rows_ref, cell_ref, lane_ref):
    for k in range(rows_ref.shape[1]):
        cell_ref[k] = rows_ref[1, k : k + 1, :].astype(jnp.int32)
        lane_ref[k] = rows_ref[2, k : k + 1, :].astype(jnp.int32)


def store_tile(ref, k, lev, low, tile, x):
    longs = ref.shape[3]
    stop = min((tile + 1) * LANES, longs)
    ref[k, lev, low : low + x.shape[0], tile * LANES : stop] = x[:, : stop - tile * LANES]


def store_four(ref, k, low, out, first, stop):
    levels = ref.shape[1]
    for t in range(first, stop):
        for lev in range(levels):
            at = ((t - first) * levels + lev) * 4
            store_tile(ref, k, lev, low, t, out[at : at + 4])


def scatter_kernel(
    rows_ref, dep_ref, part_ref, lower_ref, upper_ref, cell_ref, lane_ref, dep_row
):
    count, levels, _, longs = lower_ref.shape
    take_rows(rows_ref, cell_ref, lane_ref)
    for k in range(count):
        dep_row[k] = dep_ref[k : k + 1, :]
    tiles = -(-longs // LANES)
    high = tiles * levels * 8

    def one(k, _):
        cell = cell_ref[k].astype(jnp.int16)
        hot = jnp.concatenate(
            [one_hot(0, INNER, cell), one_hot(INNER + EDGE, OUTER - EDGE, cell)], axis=0
        )
        out = spread(hot, lane_ref[k], dep_row[k])
        for t in range(tiles):
            for lev in range(levels):
                at = (t * levels + lev) * 8
                store_tile(upper_ref, k, lev, 0, t, out[at : at + 8])
        lower_ref[k, :, :4] = part_ref[k, :, :4]
        store_four(lower_ref, k, 4, out[high:], 0, tiles)
        return 0

    lax.fori_loop(0, count, one, 0, unroll=8)


def gradient_kernel(
    last_ref,
    inc_ref,
    lat_ref,
    lon_ref,
    ew_ref,
    next_ref,
    end_low_ref,
    end_high_ref,
    previous_ref,
    lower_ref,
    upper_ref,
    below_ref,
    gram_ref,
    step_ref,
    change_ref,
    grad_ref,
    stats_ref,
    dots_ref,
):
    subs, levels, rows, longs = inc_ref.shape
    pairs = step_ref.shape[0]
    count = subs * levels
    dots_ref[...] = jnp.zeros_like(dots_ref)

    def one(j, _):
        sub, lev = j // levels, j % levels
        ew = ew_ref[lev]
        final = sub == subs - 1
        later = jnp.where(final, next_ref[lev], inc_ref[jnp.minimum(sub + 1, subs - 1), lev])
        d = ew * (later - jnp.concatenate([end_low_ref[sub, lev], end_high_ref[sub, lev]], axis=0))
        d = d * jnp.where(final, last_ref[0], 1.0)
        lat, lon = lat_ref[lev], lon_ref[lev]
        rest = 1.0 - lat - lon
        bottom = rows_of(d) == rows - 1
        for step in range(NSTEP - 1, -1, -1):
            k = sub * NSTEP + step
            d = d + jnp.concatenate([lower_ref[k, lev], upper_ref[k, lev]], axis=0)
            part = lat * d
            below = jnp.where(
                bottom, below_ref[j, step : step + 1, :], pltpu.roll(part, rows - 1, 0)
            )
            d = rest * d + below + east(lon * d)
        before = jnp.maximum(sub - 1, 0)
        before = jnp.concatenate([end_low_ref[before, lev], end_high_ref[before, lev]], axis=0)
        earlier = jnp.where(sub == 0, previous_ref[lev], before)
        g = ew * (inc_ref[sub, lev] - earlier) - d
        grad_ref[sub, lev] = g
        for i in range(pairs):
            for which, ref in enumerate((step_ref, change_ref)):
                dots_ref[which * pairs + i] += fold(g * ref[i, sub, lev].astype(F32))
        return 0

    lax.fori_loop(0, count, one, 0, unroll=2)
    sums = [jnp.sum(dots_ref[v], axis=0, keepdims=True) for v in range(2 * pairs)]
    sums = jnp.concatenate(sums, axis=0)
    dots = jnp.sum(sums, axis=1, keepdims=True)
    row, group, inner = lane_places(gram_ref.shape)
    ahead = (group - row) % pairs
    moved = jnp.concatenate([dots[pairs:], dots[:pairs]], axis=0)
    out = jnp.where(ahead == WITH_CHANGE, dots, jnp.where(ahead == WITH_STEP, moved, gram_ref[...]))
    out = jnp.where(row < pairs, gram_ref[...], out)
    stats_ref[...] = jnp.sum(jnp.where(inner == row, out, 0.0), axis=0, keepdims=True)


def fold(x):
    longs = x.shape[1]
    whole = longs - longs % LANES
    x = x[:8] + x[8:]
    out = x[:, :LANES]
    for first in range(LANES, whole, LANES):
        out = out + x[:, first : first + LANES]
    if whole < longs:
        tail = jnp.concatenate(
            [x[:, whole:], jnp.zeros((8, LANES - (longs - whole)), F32)], axis=1
        )
        out = out + tail
    return out


def direction_kernel(
    stats_ref, grad_ref, step_ref, change_ref, grad_out, direction_out, coef_ref, out_ref, sems
):
    pairs, subs, levels, _, _ = step_ref.shape
    both = 2 * pairs
    count = subs * levels
    handed = pltpu.make_async_copy(grad_ref, grad_out, sems.at[count])
    handed.start()
    stats = jnp.sum(stats_ref[...], axis=0, keepdims=True)
    shape = (both, LANES)
    row, group, inner = lane_places(shape)
    gram = jnp.broadcast_to(stats, shape)

    def column(mask, x):
        return jnp.sum(jnp.where(mask, x, 0.0), axis=1, keepdims=True)

    order = row % pairs
    changes = row >= pairs
    ahead = jnp.where(changes, WITH_CHANGE, WITH_STEP)
    dots = column((inner == pairs + order) & (group == (order + ahead) % pairs), gram)

    def with_change_of(c):
        swap = changes & ((c - order) % pairs >= WITH_CHANGE)
        return (group == jnp.where(swap, order, c)) & (inner == jnp.where(swap, pairs + c, row))

    by_change = [column(with_change_of(c), gram) for c in range(pairs)]
    by_step = [column((group == row) & (inner == i), gram)[:pairs] for i in range(pairs)]
    diagonal = column((group == row) & (inner == row), gram)[:pairs]
    rho = 1.0 / diagonal
    with_step, with_change = dots[:pairs], dots[pairs:]
    alphas = [None] * pairs
    for i in range(pairs - 1, -1, -1):
        alphas[i] = rho[i : i + 1] * with_step[i : i + 1]
        with_step = with_step - alphas[i] * by_change[i][:pairs]
        with_change = with_change - alphas[i] * by_change[i][pairs:]
    gamma = diagonal[pairs - 1 : pairs] / by_change[pairs - 1][both - 1 : both]
    with_change = gamma * with_change
    coef_ref[both] = jnp.broadcast_to(gamma, (8, LANES))
    for i in range(pairs):
        beta = rho[i : i + 1] * with_change[i : i + 1]
        rise = alphas[i] - beta
        with_change = with_change + rise * by_step[i]
        coef_ref[i] = jnp.broadcast_to(rise, (8, LANES))
        coef_ref[pairs + i] = jnp.broadcast_to(-gamma * alphas[i], (8, LANES))


    def copy(j):
        sub, lev = j // levels, j % levels
        return pltpu.make_async_copy(
            out_ref.at[sub, lev], direction_out.at[sub, lev], sems.at[j]
        )

    def one(j, _):
        sub, lev = j // levels, j % levels
        total = coef_ref[both][:1, :1] * grad_ref[sub, lev]
        for i in range(pairs):
            total += coef_ref[i][:1, :1] * step_ref[i, sub, lev].astype(F32)
            total += coef_ref[pairs + i][:1, :1] * change_ref[i, sub, lev].astype(F32)
        out_ref[sub, lev] = total
        copy(j).start()
        return 0

    lax.fori_loop(0, count, one, 0, unroll=2)
    for j in range(count):
        copy(j).wait()
    handed.wait()


def on_device(
    increment,
    forcing,
    lat_courant,
    lon_courant,
    error_weight,
    site_index,
    site_count,
    site_value,
    site_weight,
    pair_step,
    pair_change,
):
    subs, levels, rows, longs = increment.shape
    pairs = pair_step.shape[0]
    slots = site_index.shape[2]
    count = subs * levels
    wide = -(-longs // LANES) * LANES
    devices = lax.axis_size("tm") * lax.axis_size("space")
    last = jnp.where(lax.axis_index("tm") == lax.axis_size("tm") - 1, 0.0, 1.0)
    last = last.astype(F32).reshape(1)

    def like(x):
        return pltpu.VMEM(x.shape, x.dtype)

    def floats(*shape):
        return pltpu.VMEM(shape, F32)

    def far(*arrays):
        return [pltpu.with_memory_space_constraint(x, pltpu.HBM) for x in arrays]

    arguments = (increment, forcing, lat_courant, lon_courant, error_weight, site_index)
    following, edge, inc, push, lat, lon, ew, index = pl.pallas_call(
        edge_kernel,
        in_specs=[FAR] * len(arguments),
        out_specs=[WHOLE] * (2 + len(arguments)),
        out_shape=[floats(levels, rows, longs), floats(count, NSTEP, longs)]
        + [like(x) for x in arguments],
        scratch_shapes=[pltpu.SemaphoreType.DMA((len(arguments) + 5,))],
        compiler_params=params(16),
        name="edge",
    )(*far(*arguments))
    above = shifted(edge, "space", 1)
    following = shifted(following, "tm", -1)

    row_shape = (subs * NSTEP, 1, slots)
    row_scratch = [
        pltpu.VMEM(row_shape, F32),
        pltpu.VMEM(row_shape, jnp.int32),
        pltpu.VMEM(row_shape, jnp.int32),
    ]
    rows_of_slots, end_high, gram, steps, changes = pl.pallas_call(
        inner_kernel,
        in_specs=[WHOLE] * 5 + [FAR] * 2,
        out_specs=[WHOLE] * 5,
        out_shape=[
            floats(3, subs * NSTEP, slots),
            floats(subs, levels, 8, longs),
            floats(2 * pairs, pairs * rows),
            like(pair_step),
            like(pair_change),
        ],
        scratch_shapes=[
            pltpu.VMEM((subs * NSTEP, levels, rows, wide), F32),
            pltpu.VMEM((pairs * rows, 2 * pairs * rows), F32),
        ]
        + row_scratch
        + [pltpu.SemaphoreType.DMA((2, pairs))],
        compiler_params=params(28),
        name="inner",
    )(inc, push, lat, lon, index, *far(pair_step, pair_change))

    end_low, sent, edge, part, dep = pl.pallas_call(
        outer_kernel,
        in_specs=[SCALAR] + [WHOLE] * 7 + [SCALAR] + [FAR] * 2 + [WHOLE] * 2,
        out_specs=[WHOLE] * 5,
        out_shape=[
            floats(subs, levels, 8, longs),
            floats(levels, rows, longs),
            floats(count, NSTEP, longs),
            floats(subs * NSTEP, levels, 8, longs),
            floats(subs * NSTEP, slots),
        ],
        scratch_shapes=[
            pltpu.VMEM((subs * NSTEP, levels, 8, wide), F32),
            pltpu.VMEM(site_value.shape, F32),
            pltpu.VMEM(site_value.shape, F32),
        ]
        + row_scratch
        + [pltpu.VMEM(row_shape, F32), pltpu.SemaphoreType.DMA((2,))],
        compiler_params=params(24),
        name="outer",
    )(
        last,
        inc,
        push,
        lat,
        lon,
        ew,
        following,
        above,
        site_count.reshape(subs, NSTEP),
        *far(site_value, site_weight),
        rows_of_slots,
        end_high,
    )
    previous = shifted(sent, "tm", 1)
    below = shifted(edge, "space", -1)

    lower, upper = pl.pallas_call(
        scatter_kernel,
        in_specs=[WHOLE] * 3,
        out_specs=[WHOLE] * 2,
        out_shape=[floats(subs * NSTEP, levels, 8, longs)] * 2,
        scratch_shapes=row_scratch[1:] + row_scratch[:1],
        compiler_params=params(24),
        cost_estimate=pl.CostEstimate(flops=6 * 10**9, bytes_accessed=1 << 20, transcendentals=0),
        name="scatter",
    )(rows_of_slots, dep, part)

    gradient, stats = pl.pallas_call(
        gradient_kernel,
        in_specs=[SCALAR] + [WHOLE] * 14,
        out_specs=[WHOLE] * 2,
        out_shape=[like(increment), floats(1, LANES)],
        scratch_shapes=[pltpu.VMEM((2 * pairs, 8, LANES), F32)],
        compiler_params=params(16),
        name="gradient",
    )(
        last,
        inc,
        lat,
        lon,
        ew,
        following,
        end_low,
        end_high,
        previous,
        lower,
        upper,
        below,
        gram,
        steps,
        changes,
    )

    stats = jnp.broadcast_to(stats[None], (devices,) + stats.shape)
    stats = lax.all_to_all(stats, ("tm", "space"), 0, 0).reshape(devices, LANES)

    return pl.pallas_call(
        direction_kernel,
        in_specs=[WHOLE] * 4,
        out_specs=[FAR] * 2,
        out_shape=[jax.ShapeDtypeStruct(increment.shape, F32)] * 2,
        scratch_shapes=[
            pltpu.VMEM((2 * pairs + 1, 8, LANES), F32),
            pltpu.VMEM(increment.shape, F32),
            pltpu.SemaphoreType.DMA((count + 1,)),
        ],
        compiler_params=params(16),
        name="direction",
    )(stats, gradient, steps, changes)


def solution(mesh):
    return jax.shard_map(
        on_device,
        mesh=mesh,
        in_specs=(
            P("tm", None, "space", None),
            P("tm", None, "space", None),
            P(None, "space", None),
            P(None, "space", None),
            P(None, "space", None),
            P("tm", None, "space"),
            P("tm", None, "space"),
            P("tm", None, "space"),
            P("tm", None, "space"),
            P(None, "tm", None, "space", None),
            P(None, "tm", None, "space", None),
        ),
        out_specs=(P("tm", None, "space", None), P("tm", None, "space", None)),
        check_vma=False,
    )
```

```python
import functools

import jax
import jax.numpy as jnp
from jax import lax
from jax.experimental import pallas as pl
from jax.experimental.pallas import tpu as pltpu
from jax.sharding import PartitionSpec as P

NSTEP = 4
LANES = 128
F32 = jnp.float32
BF16 = jnp.bfloat16
WHOLE = pl.BlockSpec(memory_space=pltpu.VMEM)
SCALAR = pl.BlockSpec(memory_space=pltpu.SMEM)
FAR = pl.BlockSpec(memory_space=pl.ANY)


def shifted(shard, axis, by):
    count = lax.axis_size(axis)
    pairs = [(i, i + by) for i in range(count) if 0 <= i + by < count]
    return lax.ppermute(shard, axis, pairs)


def west(x):
    return jnp.concatenate([x[:, -1:], x[:, :-1]], axis=1)


def east(x):
    return jnp.concatenate([x[:, 1:], x[:, :1]], axis=1)


def rows_of(x):
    return lax.broadcasted_iota(jnp.int32, x.shape, 0)


def params(mib):
    return pltpu.CompilerParams(vmem_limit_bytes=mib << 20)


def halves(x):
    high = x.astype(BF16)
    return high, (x - high.astype(F32)).astype(BF16)


def edge_kernel(*refs):
    sources, (following_ref, edge_ref), homes, sems = refs[:5], refs[5:7], refs[7:12], refs[12]
    def lower(ref):
        return ref.at[:, :, 8:] if len(ref.shape) == 4 else ref.at[:, 8:]

    def upper(ref):
        return ref.at[:, :, :8] if len(ref.shape) == 4 else ref.at[:, :8]

    pieces = [(lower(source), lower(home)) for source, home in zip(sources[:4], homes[:4])]
    pieces += [(upper(source), upper(home)) for source, home in zip(sources[:4], homes[:4])]
    pieces += list(zip(sources[4:], homes[4:])) + [(sources[0].at[0], following_ref)]
    copies = [
        pltpu.make_async_copy(source, home, sems.at[i]) for i, (source, home) in enumerate(pieces)
    ]
    for copy in copies:
        copy.start()
    for copy in copies[:4]:
        copy.wait()
    inc_ref, forcing_ref, lat_ref, lon_ref = homes[:4]
    levels = lat_ref.shape[0]

    def one(j, _):
        sub, lev = j // levels, j % levels
        x, push = inc_ref[sub, lev, 8:], forcing_ref[sub, lev, 8:]
        lat, lon = lat_ref[lev, 8:], lon_ref[lev, 8:]
        rest = 1.0 - lat - lon
        for step in range(NSTEP):
            edge_ref[j, step : step + 1, :] = x[7:8, :]
            if step < NSTEP - 1:
                x = rest * x + lat * pltpu.roll(x, 1, 0) + lon * west(x) + push
        return 0

    lax.fori_loop(0, edge_ref.shape[0], one, 0, unroll=4)
    for copy in copies[4:]:
        copy.wait()


def pair_products(step_ref, change_ref, acc_ref, j):
    pairs, _, levels, rows, longs = step_ref.shape
    sub, lev = j // levels, j % levels
    steps = step_ref[:, sub, lev].reshape(pairs * rows, longs)
    changes = change_ref[:, sub, lev].reshape(pairs * rows, longs)
    both = jnp.concatenate([steps, changes], axis=0)
    acc_ref[...] += lax.dot_general(
        changes, both, (((1,), (1,)), ((), ())), preferred_element_type=F32
    )


def pair_sums(acc_ref, rows, out_ref):
    total = acc_ref[...].T
    row = lax.broadcasted_iota(jnp.int32, total.shape, 0)
    col = lax.broadcasted_iota(jnp.int32, total.shape, 1)
    total = jnp.where(row % rows == col % rows, total, 0.0)
    sums = [
        jnp.sum(total[first : first + rows], axis=0, keepdims=True)
        for first in range(0, total.shape[0], rows)
    ]
    sums = jnp.concatenate(sums, axis=0)
    row, group, inner = lane_places(sums.shape)
    out = jnp.zeros(sums.shape, F32)
    for c in range(sums.shape[1] // rows):
        part = jnp.sum(jnp.where(group == c, sums, 0.0), axis=1, keepdims=True)
        out = jnp.where((group == c) & (inner == row), part, out)
    out_ref[...] = out


def lane_places(shape):
    row = lax.broadcasted_iota(jnp.int32, shape, 0)
    col = lax.broadcasted_iota(jnp.int32, shape, 1)
    return row, col // shape[0], col % shape[0]


WITH_CHANGE = 5
WITH_STEP = 6


SPLIT = 8
INNER = 512
EDGE = 192
OUTER = 256


def one_hot(first, count, cell):
    place = lax.broadcasted_iota(jnp.int16, (count, cell.shape[1]), 0) + jnp.int16(first)
    return jnp.where(place == cell, jnp.ones((), BF16), jnp.zeros((), BF16))


def four_rows(ref, k, low, tile):
    lanes = slice(tile * LANES, (tile + 1) * LANES)
    return [ref[k, lev, low : low + 4, lanes] for lev in range(ref.shape[1])]


def look_up(blocks, first, cell, lane, store):
    table = jnp.concatenate(halves(jnp.concatenate([b.T for b in blocks], axis=1)), axis=0)
    chunk = 256
    for start in range(0, cell.shape[1], chunk):
        part = slice(start, start + chunk)
        hot = one_hot(first, table.shape[1], cell[:, part])
        got = jnp.dot(table, hot, preferred_element_type=F32)
        got = got[:LANES] + got[LANES:]
        mine = lax.broadcasted_iota(jnp.int32, (LANES, chunk), 0) == lane[:, part]
        store(part, jnp.sum(jnp.where(mine, got, 0.0), axis=0, keepdims=True))


def inner_kernel(
    inc_ref,
    forcing_ref,
    lat_ref,
    lon_ref,
    index_ref,
    step_far,
    change_far,
    ew_far,
    rows_ref,
    end_ref,
    gram_ref,
    step_ref,
    change_ref,
    ew_ref,
    state_ref,
    acc_ref,
    seen_ref,
    cell_ref,
    lane_ref,
    sems,
):
    subs, levels, rows, longs = inc_ref.shape
    copies = [
        pltpu.make_async_copy(far.at[i], near.at[i], sems.at[which, i])
        for i in range(step_ref.shape[0])
        for which, (far, near) in enumerate(((step_far, step_ref), (change_far, change_ref)))
    ]
    copies.append(pltpu.make_async_copy(ew_far, ew_ref, sems.at[2, 0]))
    for copy in copies:
        copy.start()
    tiles = -(-longs // LANES)
    state_ref[:, :, :, longs - longs % LANES :] = jnp.zeros(
        (subs * NSTEP, levels, rows, LANES), F32
    )
    for sub in range(subs):
        index = index_ref[sub]
        row = ((index.astype(F32) + 0.5) * (1.0 / longs)).astype(jnp.int32)
        lon = index - row * longs
        lev, lat = row // rows, row % rows
        tile, lane = lon // LANES, lon % LANES
        band = tile * 16 + lev * 4 + lat % 4
        cell = jnp.where(
            lat >= 8,
            tile * 32 + lev * 8 + lat - 8,
            jnp.where(
                lat < 4,
                INNER + band,
                jnp.where(tile < SPLIT, 384 + band, INNER + EDGE - SPLIT * 16 + band),
            ),
        )
        for step in range(NSTEP):
            k = sub * NSTEP + step
            cell_ref[k] = cell[step : step + 1]
            lane_ref[k] = lane[step : step + 1]
            rows_ref[1, k : k + 1, :] = cell[step : step + 1].astype(F32)
            rows_ref[2, k : k + 1, :] = lane[step : step + 1].astype(F32)

    def tangent(sub, lev):
        x = inc_ref[sub, lev]
        lat, lon, push = lat_ref[lev], lon_ref[lev], forcing_ref[sub, lev]
        rest = 1.0 - lat - lon
        for step in range(NSTEP):
            x = rest * x + lat * pltpu.roll(x, 1, 0) + lon * west(x) + push
            state_ref[sub * NSTEP + step, lev, :, :longs] = x
        end_ref[sub, lev] = x[8:]

    def gather(k):
        blocks = []
        for first in range(0, tiles, 4):
            part = [
                state_ref[k, :, 8:, t * LANES : (t + 1) * LANES].reshape(levels * 8, LANES)
                for t in range(first, first + 4)
            ]
            blocks.append(jnp.concatenate(part, axis=0))
        part = []
        for t in range(SPLIT):
            part += four_rows(state_ref, k, 4, t)
        blocks.append(jnp.concatenate(part, axis=0))

        def store(part, value):
            seen_ref[k, :, part] = value

        look_up(blocks, 0, cell_ref[k].astype(jnp.int16), lane_ref[k], store)

    def first(lev, _):
        tangent(0, lev)
        return 0

    lax.fori_loop(0, levels, first, 0, unroll=2)
    acc_ref[...] = jnp.zeros_like(acc_ref)

    count = subs * levels
    for i in range(NSTEP // 2):
        gather(i)
        tangent(1, 2 * i)
        tangent(1, 2 * i + 1)
    for copy in copies[:-1]:
        copy.wait()
    for i in range(NSTEP // 2):
        gather(NSTEP // 2 + i)
        pair_products(step_ref, change_ref, acc_ref, 2 * i)
        pair_products(step_ref, change_ref, acc_ref, 2 * i + 1)
    for i in range(NSTEP):
        gather(NSTEP + i)
        pair_products(step_ref, change_ref, acc_ref, count // 2 + i)
    for k in range(subs * NSTEP):
        rows_ref[0, k : k + 1, :] = seen_ref[k]
    pair_sums(acc_ref, rows, gram_ref)
    copies[-1].wait()


def outer_kernel(
    last_ref,
    inc_ref,
    forcing_ref,
    lat_ref,
    lon_ref,
    ew_ref,
    next_ref,
    above_ref,
    count_ref,
    value_far,
    weight_far,
    rows_ref,
    upper_ref,
    end_ref,
    sent_ref,
    edge_ref,
    inject_ref,
    dep_ref,
    state_ref,
    value_ref,
    weight_ref,
    seen_ref,
    cell_ref,
    lane_ref,
    dep_row,
    sems,
):
    subs, levels, _, longs = inc_ref.shape
    slots = value_ref.shape[2]
    tiles = -(-longs // LANES)
    copies = [
        pltpu.make_async_copy(value_far, value_ref, sems.at[0]),
        pltpu.make_async_copy(weight_far, weight_ref, sems.at[1]),
    ]
    for copy in copies:
        copy.start()
    state_ref[:, :, :, longs - longs % LANES :] = jnp.zeros((subs * NSTEP, levels, 8, LANES), F32)
    take_rows(rows_ref, cell_ref, lane_ref)

    def tangent(sub, lev):
        j = sub * levels + lev
        x, push = inc_ref[sub, lev, :8], forcing_ref[sub, lev, :8]
        lat, lon = lat_ref[lev, :8], lon_ref[lev, :8]
        rest = 1.0 - lat - lon
        top = rows_of(x) == 0
        for step in range(NSTEP):
            above = jnp.where(top, above_ref[j, step : step + 1, :], pltpu.roll(x, 1, 0))
            x = rest * x + lat * above + lon * west(x) + push
            state_ref[sub * NSTEP + step, lev, :, :longs] = x
        end_ref[sub, lev] = x
        if sub == subs - 1:
            sent_ref[lev, :8] = x
            sent_ref[lev, 8:] = upper_ref[sub, lev]

    def gather(k):
        part = []
        for t in range(tiles):
            part += four_rows(state_ref, k, 0, t)
        for t in range(SPLIT, tiles):
            part += four_rows(state_ref, k, 4, t)
        half = len(part) // 2
        blocks = [jnp.concatenate(part[:half], axis=0), jnp.concatenate(part[half:], axis=0)]

        def store(part, value):
            seen_ref[k, :, part] = value

        look_up(blocks, INNER, cell_ref[k].astype(jnp.int16), lane_ref[k], store)

    slot = lax.broadcasted_iota(jnp.int32, (NSTEP, slots), 1)
    row = lax.broadcasted_iota(jnp.int32, (NSTEP, slots), 0)

    def departures(sub):
        ks = range(sub * NSTEP, (sub + 1) * NSTEP)
        seen = rows_ref[0, ks.start : ks.stop, :]
        seen = seen + jnp.concatenate([seen_ref[k] for k in ks], axis=0)
        live = slot < 0
        for step in range(NSTEP):
            live = live | ((row == step) & (slot < count_ref[sub, step]))
        dep = jnp.where(live, weight_ref[sub] * (value_ref[sub] - seen), 0.0)
        dep_ref[ks.start : ks.stop, :] = dep
        for step in range(NSTEP):
            dep_row[ks[step]] = dep[step : step + 1]

    def scatter(k):
        cell = cell_ref[k].astype(jnp.int16)
        out = spread(one_hot(INNER, EDGE, cell), lane_ref[k], dep_row[k])
        store_four(inject_ref, k, 0, out, 0, tiles)

    def dual_edge(sub, lev):
        j = sub * levels + lev
        later = next_ref[lev, :8] if sub == subs - 1 else inc_ref[sub + 1, lev, :8]
        d = ew_ref[lev, :8] * (later - end_ref[sub, lev])
        if sub == subs - 1:
            d = d * last_ref[0]
        lat, lon = lat_ref[lev, :8], lon_ref[lev, :8]
        rest = 1.0 - lat - lon
        for step in range(NSTEP - 1, -1, -1):
            d = d + inject_ref[sub * NSTEP + step, lev]
            part = lat * d
            edge_ref[j, step : step + 1, :] = part[:1, :]
            if step:
                d = rest * d + pltpu.roll(part, 7, 0) + east(lon * d)

    for lev in range(levels):
        tangent(0, lev)
    for i in range(NSTEP):
        gather(i)
        tangent(1, i)
    for copy in copies:
        copy.wait()
    departures(0)
    for i in range(NSTEP):
        gather(NSTEP + i)
        scatter(i)
    departures(1)
    for i in range(NSTEP):
        scatter(NSTEP + i)
        dual_edge(0, i)
    for lev in range(levels):
        dual_edge(1, lev)


def spread(hot, lane, dep):
    high, low = halves(dep)
    mine = lax.broadcasted_iota(jnp.int16, (LANES, dep.shape[1]), 0) == lane.astype(jnp.int16)
    zero = jnp.zeros((), BF16)
    values = jnp.concatenate([jnp.where(mine, high, zero), jnp.where(mine, low, zero)], axis=0)
    out = lax.dot_general(hot, values, (((1,), (1,)), ((), ())), preferred_element_type=F32)
    return out[:, :LANES] + out[:, LANES:]


def take_rows(rows_ref, cell_ref, lane_ref):
    for k in range(rows_ref.shape[1]):
        cell_ref[k] = rows_ref[1, k : k + 1, :].astype(jnp.int32)
        lane_ref[k] = rows_ref[2, k : k + 1, :].astype(jnp.int32)


def store_tile(ref, k, lev, low, tile, x):
    longs = ref.shape[3]
    stop = min((tile + 1) * LANES, longs)
    ref[k, lev, low : low + x.shape[0], tile * LANES : stop] = x[:, : stop - tile * LANES]


def store_four(ref, k, low, out, first, stop):
    levels = ref.shape[1]
    for t in range(first, stop):
        for lev in range(levels):
            at = ((t - first) * levels + lev) * 4
            store_tile(ref, k, lev, low, t, out[at : at + 4])


def scatter_kernel(
    rows_ref, dep_ref, part_ref, lower_ref, upper_ref, cell_ref, lane_ref, dep_row
):
    count, levels, _, longs = lower_ref.shape
    take_rows(rows_ref, cell_ref, lane_ref)
    for k in range(count):
        dep_row[k] = dep_ref[k : k + 1, :]
    tiles = -(-longs // LANES)
    high = tiles * levels * 8

    def one(k, _):
        cell = cell_ref[k].astype(jnp.int16)
        hot = jnp.concatenate(
            [one_hot(0, INNER, cell), one_hot(INNER + EDGE, OUTER - EDGE, cell)], axis=0
        )
        out = spread(hot, lane_ref[k], dep_row[k])
        for t in range(tiles):
            for lev in range(levels):
                at = (t * levels + lev) * 8
                store_tile(upper_ref, k, lev, 0, t, out[at : at + 8])
        lower_ref[k, :, :4] = part_ref[k, :, :4]
        store_four(lower_ref, k, 4, out[high:], 0, tiles)
        return 0

    lax.fori_loop(0, count, one, 0, unroll=8)


def add_gradient(
    sub,
    last_ref,
    inc_ref,
    lat_ref,
    lon_ref,
    ew_ref,
    later_ref,
    earlier_ref,
    end_low_ref,
    end_high_ref,
    lower_ref,
    upper_ref,
    below_ref,
    step_ref,
    change_ref,
    grad_ref,
    dots_ref,
):
    subs, levels, rows, longs = inc_ref.shape
    pairs = step_ref.shape[0]

    def one(lev, _):
        ew = ew_ref[lev]
        end = jnp.concatenate([end_low_ref[sub, lev], end_high_ref[sub, lev]], axis=0)
        if sub == subs - 1:
            d = ew * (later_ref[lev] - end) * last_ref[0]
        else:
            d = ew * (inc_ref[sub + 1, lev] - end)
        lat, lon = lat_ref[lev], lon_ref[lev]
        rest = 1.0 - lat - lon
        bottom = rows_of(d) == rows - 1
        for step in range(NSTEP - 1, -1, -1):
            k = sub * NSTEP + step
            d = d + jnp.concatenate([lower_ref[k, lev], upper_ref[k, lev]], axis=0)
            part = lat * d
            below = below_ref[sub * levels + lev, step : step + 1, :]
            below = jnp.where(bottom, below, pltpu.roll(part, rows - 1, 0))
            d = rest * d + below + east(lon * d)
        if sub == 0:
            earlier = earlier_ref[lev]
        else:
            earlier = jnp.concatenate(
                [end_low_ref[sub - 1, lev], end_high_ref[sub - 1, lev]], axis=0
            )
        g = ew * (inc_ref[sub, lev] - earlier) - d
        grad_ref[lev] = g
        for i in range(pairs):
            for which, ref in enumerate((step_ref, change_ref)):
                dots_ref[which * pairs + i] += fold(g * ref[i, sub, lev].astype(F32))
        return 0

    lax.fori_loop(0, levels, one, 0, unroll=2)


def second_kernel(last_ref, inc_ref, lat_ref, lon_ref, ew_ref, next_ref, *refs):
    dots_ref = refs[-1]
    dots_ref[...] = jnp.zeros_like(dots_ref)
    sub = inc_ref.shape[0] - 1
    add_gradient(sub, last_ref, inc_ref, lat_ref, lon_ref, ew_ref, next_ref, None, *refs)


def first_kernel(inc_ref, lat_ref, lon_ref, ew_ref, previous_ref, *refs):
    dots_in, gram_ref, grad_ref, stats_ref, dots_ref = refs[-5:]
    pairs = gram_ref.shape[0] // 2
    dots_ref[...] = dots_in[...]
    add_gradient(
        0,
        None,
        inc_ref,
        lat_ref,
        lon_ref,
        ew_ref,
        None,
        previous_ref,
        *refs[:-5],
        grad_ref,
        dots_ref,
    )
    sums = [jnp.sum(dots_ref[v], axis=0, keepdims=True) for v in range(2 * pairs)]
    sums = jnp.concatenate(sums, axis=0)
    dots = jnp.sum(sums, axis=1, keepdims=True)
    row, group, inner = lane_places(gram_ref.shape)
    ahead = (group - row) % pairs
    moved = jnp.concatenate([dots[pairs:], dots[:pairs]], axis=0)
    out = jnp.where(ahead == WITH_CHANGE, dots, jnp.where(ahead == WITH_STEP, moved, gram_ref[...]))
    out = jnp.where(row < pairs, gram_ref[...], out)
    stats_ref[...] = jnp.sum(jnp.where(inner == row, out, 0.0), axis=0, keepdims=True)


def fold(x):
    longs = x.shape[1]
    whole = longs - longs % LANES
    x = x[:8] + x[8:]
    out = x[:, :LANES]
    for first in range(LANES, whole, LANES):
        out = out + x[:, first : first + LANES]
    if whole < longs:
        tail = jnp.concatenate(
            [x[:, whole:], jnp.zeros((8, LANES - (longs - whole)), F32)], axis=1
        )
        out = out + tail
    return out


def direction_kernel(
    stats_ref, first_ref, second_ref, step_ref, change_ref, grad_out, direction_out, coef_ref,
    out_ref, sems,
):
    pairs, subs, levels, _, _ = step_ref.shape
    both = 2 * pairs
    count = subs * levels
    grads = (first_ref, second_ref)
    handed = [
        pltpu.make_async_copy(ref, grad_out.at[sub], sems.at[count + sub])
        for sub, ref in enumerate(grads)
    ]
    for copy in handed:
        copy.start()
    stats = jnp.sum(stats_ref[...], axis=0, keepdims=True)
    shape = (both, LANES)
    row, group, inner = lane_places(shape)
    gram = jnp.broadcast_to(stats, shape)

    def column(mask, x):
        return jnp.sum(jnp.where(mask, x, 0.0), axis=1, keepdims=True)

    order = row % pairs
    changes = row >= pairs
    ahead = jnp.where(changes, WITH_CHANGE, WITH_STEP)
    dots = column((inner == pairs + order) & (group == (order + ahead) % pairs), gram)

    def with_change_of(c):
        swap = changes & ((c - order) % pairs >= WITH_CHANGE)
        return (group == jnp.where(swap, order, c)) & (inner == jnp.where(swap, pairs + c, row))

    by_change = [column(with_change_of(c), gram) for c in range(pairs)]
    by_step = [column((group == row) & (inner == i), gram)[:pairs] for i in range(pairs)]
    diagonal = column((group == row) & (inner == row), gram)[:pairs]
    rho = 1.0 / diagonal
    with_step, with_change = dots[:pairs], dots[pairs:]
    alphas = [None] * pairs
    for i in range(pairs - 1, -1, -1):
        alphas[i] = rho[i : i + 1] * with_step[i : i + 1]
        with_step = with_step - alphas[i] * by_change[i][:pairs]
        with_change = with_change - alphas[i] * by_change[i][pairs:]
    gamma = diagonal[pairs - 1 : pairs] / by_change[pairs - 1][both - 1 : both]
    with_change = gamma * with_change
    coef_ref[both] = jnp.broadcast_to(gamma, (8, LANES))
    for i in range(pairs):
        beta = rho[i : i + 1] * with_change[i : i + 1]
        rise = alphas[i] - beta
        with_change = with_change + rise * by_step[i]
        coef_ref[i] = jnp.broadcast_to(rise, (8, LANES))
        coef_ref[pairs + i] = jnp.broadcast_to(-gamma * alphas[i], (8, LANES))


    copies = []
    for sub in range(subs):
        for lev in range(levels):
            total = coef_ref[both][:1, :1] * grads[sub][lev]
            for i in range(pairs):
                total += coef_ref[i][:1, :1] * step_ref[i, sub, lev].astype(F32)
                total += coef_ref[pairs + i][:1, :1] * change_ref[i, sub, lev].astype(F32)
            out_ref[sub, lev] = total
            copies.append(
                pltpu.make_async_copy(
                    out_ref.at[sub, lev], direction_out.at[sub, lev], sems.at[len(copies)]
                )
            )
            copies[-1].start()
    for copy in copies + handed:
        copy.wait()


def on_device(
    increment,
    forcing,
    lat_courant,
    lon_courant,
    error_weight,
    site_index,
    site_count,
    site_value,
    site_weight,
    pair_step,
    pair_change,
):
    subs, levels, rows, longs = increment.shape
    pairs = pair_step.shape[0]
    slots = site_index.shape[2]
    count = subs * levels
    wide = -(-longs // LANES) * LANES
    devices = lax.axis_size("tm") * lax.axis_size("space")
    last = jnp.where(lax.axis_index("tm") == lax.axis_size("tm") - 1, 0.0, 1.0)
    last = last.astype(F32).reshape(1)

    def like(x):
        return pltpu.VMEM(x.shape, x.dtype)

    def floats(*shape):
        return pltpu.VMEM(shape, F32)

    def far(*arrays):
        return [pltpu.with_memory_space_constraint(x, pltpu.HBM) for x in arrays]

    arguments = (increment, forcing, lat_courant, lon_courant, site_index)
    following, edge, inc, push, lat, lon, index = pl.pallas_call(
        edge_kernel,
        in_specs=[FAR] * len(arguments),
        out_specs=[WHOLE] * (2 + len(arguments)),
        out_shape=[floats(levels, rows, longs), floats(count, NSTEP, longs)]
        + [like(x) for x in arguments],
        scratch_shapes=[pltpu.SemaphoreType.DMA((len(arguments) + 5,))],
        compiler_params=params(16),
        name="edge",
    )(*far(*arguments))
    above = shifted(edge, "space", 1)
    following = shifted(following, "tm", -1)

    row_shape = (subs * NSTEP, 1, slots)
    row_scratch = [
        pltpu.VMEM(row_shape, F32),
        pltpu.VMEM(row_shape, jnp.int32),
        pltpu.VMEM(row_shape, jnp.int32),
    ]
    rows_of_slots, end_high, gram, steps, changes, ew = pl.pallas_call(
        inner_kernel,
        in_specs=[WHOLE] * 5 + [FAR] * 3,
        out_specs=[WHOLE] * 6,
        out_shape=[
            floats(3, subs * NSTEP, slots),
            floats(subs, levels, 8, longs),
            floats(2 * pairs, pairs * rows),
            like(pair_step),
            like(pair_change),
            like(error_weight),
        ],
        scratch_shapes=[
            pltpu.VMEM((subs * NSTEP, levels, rows, wide), F32),
            pltpu.VMEM((pairs * rows, 2 * pairs * rows), F32),
        ]
        + row_scratch
        + [pltpu.SemaphoreType.DMA((3, pairs))],
        compiler_params=params(28),
        name="inner",
    )(inc, push, lat, lon, index, *far(pair_step, pair_change, error_weight))

    end_low, sent, edge, part, dep = pl.pallas_call(
        outer_kernel,
        in_specs=[SCALAR] + [WHOLE] * 7 + [SCALAR] + [FAR] * 2 + [WHOLE] * 2,
        out_specs=[WHOLE] * 5,
        out_shape=[
            floats(subs, levels, 8, longs),
            floats(levels, rows, longs),
            floats(count, NSTEP, longs),
            floats(subs * NSTEP, levels, 8, longs),
            floats(subs * NSTEP, slots),
        ],
        scratch_shapes=[
            pltpu.VMEM((subs * NSTEP, levels, 8, wide), F32),
            pltpu.VMEM(site_value.shape, F32),
            pltpu.VMEM(site_value.shape, F32),
        ]
        + row_scratch
        + [pltpu.VMEM(row_shape, F32), pltpu.SemaphoreType.DMA((2,))],
        compiler_params=params(24),
        name="outer",
    )(
        last,
        inc,
        push,
        lat,
        lon,
        ew,
        following,
        above,
        site_count.reshape(subs, NSTEP),
        *far(site_value, site_weight),
        rows_of_slots,
        end_high,
    )
    previous = shifted(sent, "tm", 1)
    below = shifted(edge, "space", -1)

    lower, upper = pl.pallas_call(
        scatter_kernel,
        in_specs=[WHOLE] * 3,
        out_specs=[WHOLE] * 2,
        out_shape=[floats(subs * NSTEP, levels, 8, longs)] * 2,
        scratch_shapes=row_scratch[1:] + row_scratch[:1],
        compiler_params=params(24),
        cost_estimate=pl.CostEstimate(flops=6 * 10**9, bytes_accessed=1 << 20, transcendentals=0),
        name="scatter",
    )(rows_of_slots, dep, part)

    shared = (end_low, end_high, lower, upper, below, steps, changes)
    grad_second, dots = pl.pallas_call(
        second_kernel,
        in_specs=[SCALAR] + [WHOLE] * 12,
        out_specs=[WHOLE] * 2,
        out_shape=[floats(levels, rows, longs), floats(2 * pairs, 8, LANES)],
        compiler_params=params(16),
        name="second",
    )(last, inc, lat, lon, ew, following, *shared)
    grad_first, stats = pl.pallas_call(
        first_kernel,
        in_specs=[WHOLE] * 14,
        out_specs=[WHOLE] * 2,
        out_shape=[floats(levels, rows, longs), floats(1, LANES)],
        scratch_shapes=[pltpu.VMEM((2 * pairs, 8, LANES), F32)],
        compiler_params=params(16),
        name="first",
    )(inc, lat, lon, ew, previous, *shared, dots, gram)

    stats = jnp.broadcast_to(stats[None], (devices,) + stats.shape)
    stats = lax.all_to_all(stats, ("tm", "space"), 0, 0).reshape(devices, LANES)

    return pl.pallas_call(
        direction_kernel,
        in_specs=[WHOLE] * 5,
        out_specs=[FAR] * 2,
        out_shape=[jax.ShapeDtypeStruct(increment.shape, F32)] * 2,
        scratch_shapes=[
            pltpu.VMEM((2 * pairs + 1, 8, LANES), F32),
            pltpu.VMEM(increment.shape, F32),
            pltpu.SemaphoreType.DMA((count + subs,)),
        ],
        compiler_params=params(16),
        name="direction",
    )(stats, grad_first, grad_second, steps, changes)


def solution(mesh):
    return jax.shard_map(
        on_device,
        mesh=mesh,
        in_specs=(
            P("tm", None, "space", None),
            P("tm", None, "space", None),
            P(None, "space", None),
            P(None, "space", None),
            P(None, "space", None),
            P("tm", None, "space"),
            P("tm", None, "space"),
            P("tm", None, "space"),
            P("tm", None, "space"),
            P(None, "tm", None, "space", None),
            P(None, "tm", None, "space", None),
        ),
        out_specs=(P("tm", None, "space", None), P("tm", None, "space", None)),
        check_vma=False,
    )
```

```python
import functools

import jax
import jax.numpy as jnp
from jax import lax
from jax.experimental import pallas as pl
from jax.experimental.pallas import tpu as pltpu
from jax.sharding import PartitionSpec as P

NSTEP = 4
LANES = 128
F32 = jnp.float32
BF16 = jnp.bfloat16
WHOLE = pl.BlockSpec(memory_space=pltpu.VMEM)
SCALAR = pl.BlockSpec(memory_space=pltpu.SMEM)
FAR = pl.BlockSpec(memory_space=pl.ANY)


def shifted(shard, axis, by):
    count = lax.axis_size(axis)
    pairs = [(i, i + by) for i in range(count) if 0 <= i + by < count]
    return lax.ppermute(shard, axis, pairs)


def west(x):
    return jnp.concatenate([x[:, -1:], x[:, :-1]], axis=1)


def east(x):
    return jnp.concatenate([x[:, 1:], x[:, :1]], axis=1)


def rows_of(x):
    return lax.broadcasted_iota(jnp.int32, x.shape, 0)


def params(mib):
    return pltpu.CompilerParams(vmem_limit_bytes=mib << 20)


def halves(x):
    high = x.astype(BF16)
    return high, (x - high.astype(F32)).astype(BF16)


def edge_kernel(*refs):
    sources, (following_ref, edge_ref), homes, sems = refs[:5], refs[5:7], refs[7:12], refs[12]
    def lower(ref):
        return ref.at[:, :, 8:] if len(ref.shape) == 4 else ref.at[:, 8:]

    def upper(ref):
        return ref.at[:, :, :8] if len(ref.shape) == 4 else ref.at[:, :8]

    pieces = [(lower(source), lower(home)) for source, home in zip(sources[:4], homes[:4])]
    pieces += [(upper(source), upper(home)) for source, home in zip(sources[:4], homes[:4])]
    pieces += list(zip(sources[4:], homes[4:])) + [(sources[0].at[0], following_ref)]
    copies = [
        pltpu.make_async_copy(source, home, sems.at[i]) for i, (source, home) in enumerate(pieces)
    ]
    for copy in copies:
        copy.start()
    for copy in copies[:4]:
        copy.wait()
    inc_ref, forcing_ref, lat_ref, lon_ref = homes[:4]
    levels = lat_ref.shape[0]

    def one(j, _):
        sub, lev = j // levels, j % levels
        x, push = inc_ref[sub, lev, 8:], forcing_ref[sub, lev, 8:]
        lat, lon = lat_ref[lev, 8:], lon_ref[lev, 8:]
        rest = 1.0 - lat - lon
        for step in range(NSTEP):
            edge_ref[j, step : step + 1, :] = x[7:8, :]
            if step < NSTEP - 1:
                x = rest * x + lat * pltpu.roll(x, 1, 0) + lon * west(x) + push
        return 0

    lax.fori_loop(0, edge_ref.shape[0], one, 0, unroll=4)
    for copy in copies[4:]:
        copy.wait()


def pair_products(step_ref, change_ref, acc_ref, j):
    pairs, _, levels, rows, longs = step_ref.shape
    sub, lev = j // levels, j % levels
    steps = step_ref[:, sub, lev].reshape(pairs * rows, longs)
    changes = change_ref[:, sub, lev].reshape(pairs * rows, longs)
    both = jnp.concatenate([steps, changes], axis=0)
    acc_ref[...] += lax.dot_general(
        changes, both, (((1,), (1,)), ((), ())), preferred_element_type=F32
    )


def pair_sums(acc_ref, rows, out_ref):
    total = acc_ref[...].T
    row = lax.broadcasted_iota(jnp.int32, total.shape, 0)
    col = lax.broadcasted_iota(jnp.int32, total.shape, 1)
    total = jnp.where(row % rows == col % rows, total, 0.0)
    sums = [
        jnp.sum(total[first : first + rows], axis=0, keepdims=True)
        for first in range(0, total.shape[0], rows)
    ]
    sums = jnp.concatenate(sums, axis=0)
    row, group, inner = lane_places(sums.shape)
    out = jnp.zeros(sums.shape, F32)
    for c in range(sums.shape[1] // rows):
        part = jnp.sum(jnp.where(group == c, sums, 0.0), axis=1, keepdims=True)
        out = jnp.where((group == c) & (inner == row), part, out)
    out_ref[...] = out


def lane_places(shape):
    row = lax.broadcasted_iota(jnp.int32, shape, 0)
    col = lax.broadcasted_iota(jnp.int32, shape, 1)
    return row, col // shape[0], col % shape[0]


WITH_CHANGE = 5
WITH_STEP = 6


SPLIT = 8
INNER = 512
EDGE = 192
OUTER = 256


def one_hot(first, count, cell):
    place = lax.broadcasted_iota(jnp.int16, (count, cell.shape[1]), 0) + jnp.int16(first)
    return jnp.where(place == cell, jnp.ones((), BF16), jnp.zeros((), BF16))


def four_rows(ref, k, low, tile):
    lanes = slice(tile * LANES, (tile + 1) * LANES)
    return [ref[k, lev, low : low + 4, lanes] for lev in range(ref.shape[1])]


def look_up(blocks, first, cell, lane, store):
    table = jnp.concatenate(halves(jnp.concatenate([b.T for b in blocks], axis=1)), axis=0)
    chunk = 256
    for start in range(0, cell.shape[1], chunk):
        part = slice(start, start + chunk)
        hot = one_hot(first, table.shape[1], cell[:, part])
        got = jnp.dot(table, hot, preferred_element_type=F32)
        got = got[:LANES] + got[LANES:]
        mine = lax.broadcasted_iota(jnp.int32, (LANES, chunk), 0) == lane[:, part]
        store(part, jnp.sum(jnp.where(mine, got, 0.0), axis=0, keepdims=True))


def inner_kernel(
    inc_ref,
    forcing_ref,
    lat_ref,
    lon_ref,
    index_ref,
    step_far,
    change_far,
    ew_far,
    rows_ref,
    end_ref,
    step_ref,
    change_ref,
    ew_ref,
    state_ref,
    seen_ref,
    cell_ref,
    lane_ref,
    sems,
):
    subs, levels, rows, longs = inc_ref.shape
    copies = [
        pltpu.make_async_copy(far.at[i], near.at[i], sems.at[which, i])
        for i in range(step_ref.shape[0])
        for which, (far, near) in enumerate(((step_far, step_ref), (change_far, change_ref)))
    ]
    copies.append(pltpu.make_async_copy(ew_far, ew_ref, sems.at[2, 0]))
    for copy in copies:
        copy.start()
    tiles = -(-longs // LANES)
    state_ref[:, :, :, longs - longs % LANES :] = jnp.zeros(
        (subs * NSTEP, levels, rows, LANES), F32
    )
    for sub in range(subs):
        index = index_ref[sub]
        row = ((index.astype(F32) + 0.5) * (1.0 / longs)).astype(jnp.int32)
        lon = index - row * longs
        lev, lat = row // rows, row % rows
        tile, lane = lon // LANES, lon % LANES
        band = tile * 16 + lev * 4 + lat % 4
        cell = jnp.where(
            lat >= 8,
            tile * 32 + lev * 8 + lat - 8,
            jnp.where(
                lat < 4,
                INNER + band,
                jnp.where(tile < SPLIT, 384 + band, INNER + EDGE - SPLIT * 16 + band),
            ),
        )
        for step in range(NSTEP):
            k = sub * NSTEP + step
            cell_ref[k] = cell[step : step + 1]
            lane_ref[k] = lane[step : step + 1]
            rows_ref[1, k : k + 1, :] = cell[step : step + 1].astype(F32)
            rows_ref[2, k : k + 1, :] = lane[step : step + 1].astype(F32)

    def tangent(sub, lev):
        x = inc_ref[sub, lev]
        lat, lon, push = lat_ref[lev], lon_ref[lev], forcing_ref[sub, lev]
        rest = 1.0 - lat - lon
        for step in range(NSTEP):
            x = rest * x + lat * pltpu.roll(x, 1, 0) + lon * west(x) + push
            state_ref[sub * NSTEP + step, lev, :, :longs] = x
        end_ref[sub, lev] = x[8:]

    def gather(k):
        blocks = []
        for first in range(0, tiles, 4):
            part = [
                state_ref[k, :, 8:, t * LANES : (t + 1) * LANES].reshape(levels * 8, LANES)
                for t in range(first, first + 4)
            ]
            blocks.append(jnp.concatenate(part, axis=0))
        part = []
        for t in range(SPLIT):
            part += four_rows(state_ref, k, 4, t)
        blocks.append(jnp.concatenate(part, axis=0))

        def store(part, value):
            seen_ref[k, :, part] = value

        look_up(blocks, 0, cell_ref[k].astype(jnp.int16), lane_ref[k], store)

    def first(lev, _):
        tangent(0, lev)
        return 0

    lax.fori_loop(0, levels, first, 0, unroll=2)
    for i in range(NSTEP // 2):
        gather(i)
        tangent(1, 2 * i)
        tangent(1, 2 * i + 1)
    for i in range(NSTEP // 2):
        gather(NSTEP // 2 + i)
    for i in range(NSTEP):
        gather(NSTEP + i)
    for k in range(subs * NSTEP):
        rows_ref[0, k : k + 1, :] = seen_ref[k]
    for copy in copies:
        copy.wait()


def outer_kernel(
    last_ref,
    inc_ref,
    forcing_ref,
    lat_ref,
    lon_ref,
    ew_ref,
    next_ref,
    above_ref,
    count_ref,
    value_far,
    weight_far,
    rows_ref,
    upper_ref,
    end_ref,
    sent_ref,
    edge_ref,
    inject_ref,
    dep_ref,
    state_ref,
    value_ref,
    weight_ref,
    seen_ref,
    cell_ref,
    lane_ref,
    dep_row,
    sems,
):
    subs, levels, _, longs = inc_ref.shape
    slots = value_ref.shape[2]
    tiles = -(-longs // LANES)
    copies = [
        pltpu.make_async_copy(value_far, value_ref, sems.at[0]),
        pltpu.make_async_copy(weight_far, weight_ref, sems.at[1]),
    ]
    for copy in copies:
        copy.start()
    state_ref[:, :, :, longs - longs % LANES :] = jnp.zeros((subs * NSTEP, levels, 8, LANES), F32)
    take_rows(rows_ref, cell_ref, lane_ref)

    def tangent(sub, lev):
        j = sub * levels + lev
        x, push = inc_ref[sub, lev, :8], forcing_ref[sub, lev, :8]
        lat, lon = lat_ref[lev, :8], lon_ref[lev, :8]
        rest = 1.0 - lat - lon
        top = rows_of(x) == 0
        for step in range(NSTEP):
            above = jnp.where(top, above_ref[j, step : step + 1, :], pltpu.roll(x, 1, 0))
            x = rest * x + lat * above + lon * west(x) + push
            state_ref[sub * NSTEP + step, lev, :, :longs] = x
        end_ref[sub, lev] = x
        if sub == subs - 1:
            sent_ref[lev, :8] = x
            sent_ref[lev, 8:] = upper_ref[sub, lev]

    def gather(k):
        part = []
        for t in range(tiles):
            part += four_rows(state_ref, k, 0, t)
        for t in range(SPLIT, tiles):
            part += four_rows(state_ref, k, 4, t)
        half = len(part) // 2
        blocks = [jnp.concatenate(part[:half], axis=0), jnp.concatenate(part[half:], axis=0)]

        def store(part, value):
            seen_ref[k, :, part] = value

        look_up(blocks, INNER, cell_ref[k].astype(jnp.int16), lane_ref[k], store)

    slot = lax.broadcasted_iota(jnp.int32, (NSTEP, slots), 1)
    row = lax.broadcasted_iota(jnp.int32, (NSTEP, slots), 0)

    def departures(sub):
        ks = range(sub * NSTEP, (sub + 1) * NSTEP)
        seen = rows_ref[0, ks.start : ks.stop, :]
        seen = seen + jnp.concatenate([seen_ref[k] for k in ks], axis=0)
        live = slot < 0
        for step in range(NSTEP):
            live = live | ((row == step) & (slot < count_ref[sub, step]))
        dep = jnp.where(live, weight_ref[sub] * (value_ref[sub] - seen), 0.0)
        dep_ref[ks.start : ks.stop, :] = dep
        for step in range(NSTEP):
            dep_row[ks[step]] = dep[step : step + 1]

    def scatter(k):
        cell = cell_ref[k].astype(jnp.int16)
        out = spread(one_hot(INNER, EDGE, cell), lane_ref[k], dep_row[k])
        store_four(inject_ref, k, 0, out, 0, tiles)

    def dual_edge(sub, lev):
        j = sub * levels + lev
        later = next_ref[lev, :8] if sub == subs - 1 else inc_ref[sub + 1, lev, :8]
        d = ew_ref[lev, :8] * (later - end_ref[sub, lev])
        if sub == subs - 1:
            d = d * last_ref[0]
        lat, lon = lat_ref[lev, :8], lon_ref[lev, :8]
        rest = 1.0 - lat - lon
        for step in range(NSTEP - 1, -1, -1):
            d = d + inject_ref[sub * NSTEP + step, lev]
            part = lat * d
            edge_ref[j, step : step + 1, :] = part[:1, :]
            if step:
                d = rest * d + pltpu.roll(part, 7, 0) + east(lon * d)

    for lev in range(levels):
        tangent(0, lev)
    for i in range(NSTEP):
        gather(i)
        tangent(1, i)
    for copy in copies:
        copy.wait()
    departures(0)
    for i in range(NSTEP):
        gather(NSTEP + i)
        scatter(i)
    departures(1)
    for i in range(NSTEP):
        scatter(NSTEP + i)
        dual_edge(0, i)
    for lev in range(levels):
        dual_edge(1, lev)


def spread(hot, lane, dep):
    high, low = halves(dep)
    mine = lax.broadcasted_iota(jnp.int16, (LANES, dep.shape[1]), 0) == lane.astype(jnp.int16)
    zero = jnp.zeros((), BF16)
    values = jnp.concatenate([jnp.where(mine, high, zero), jnp.where(mine, low, zero)], axis=0)
    out = lax.dot_general(hot, values, (((1,), (1,)), ((), ())), preferred_element_type=F32)
    return out[:, :LANES] + out[:, LANES:]


def take_rows(rows_ref, cell_ref, lane_ref):
    for k in range(rows_ref.shape[1]):
        cell_ref[k] = rows_ref[1, k : k + 1, :].astype(jnp.int32)
        lane_ref[k] = rows_ref[2, k : k + 1, :].astype(jnp.int32)


def store_tile(ref, k, lev, low, tile, x):
    longs = ref.shape[3]
    stop = min((tile + 1) * LANES, longs)
    ref[k, lev, low : low + x.shape[0], tile * LANES : stop] = x[:, : stop - tile * LANES]


def store_four(ref, k, low, out, first, stop):
    levels = ref.shape[1]
    for t in range(first, stop):
        for lev in range(levels):
            at = ((t - first) * levels + lev) * 4
            store_tile(ref, k, lev, low, t, out[at : at + 4])


def scatter_kernel(
    rows_ref, dep_ref, part_ref, lower_ref, upper_ref, cell_ref, lane_ref, dep_row
):
    count, levels, _, longs = lower_ref.shape
    take_rows(rows_ref, cell_ref, lane_ref)
    for k in range(count):
        dep_row[k] = dep_ref[k : k + 1, :]
    tiles = -(-longs // LANES)
    high = tiles * levels * 8

    def one(k, _):
        cell = cell_ref[k].astype(jnp.int16)
        hot = jnp.concatenate(
            [one_hot(0, INNER, cell), one_hot(INNER + EDGE, OUTER - EDGE, cell)], axis=0
        )
        out = spread(hot, lane_ref[k], dep_row[k])
        for t in range(tiles):
            for lev in range(levels):
                at = (t * levels + lev) * 8
                store_tile(upper_ref, k, lev, 0, t, out[at : at + 8])
        lower_ref[k, :, :4] = part_ref[k, :, :4]
        store_four(lower_ref, k, 4, out[high:], 0, tiles)
        return 0

    lax.fori_loop(0, count, one, 0, unroll=8)


def add_gradient(
    sub,
    last_ref,
    inc_ref,
    lat_ref,
    lon_ref,
    ew_ref,
    later_ref,
    earlier_ref,
    end_low_ref,
    end_high_ref,
    lower_ref,
    upper_ref,
    below_ref,
    step_ref,
    change_ref,
    grad_ref,
    dots_ref,
    beside=None,
):
    subs, levels, rows, longs = inc_ref.shape
    pairs = step_ref.shape[0]

    def one(lev, _):
        if beside is not None:
            beside(lev)
        ew = ew_ref[lev]
        end = jnp.concatenate([end_low_ref[sub, lev], end_high_ref[sub, lev]], axis=0)
        if sub == subs - 1:
            d = ew * (later_ref[lev] - end) * last_ref[0]
        else:
            d = ew * (inc_ref[sub + 1, lev] - end)
        lat, lon = lat_ref[lev], lon_ref[lev]
        rest = 1.0 - lat - lon
        bottom = rows_of(d) == rows - 1
        for step in range(NSTEP - 1, -1, -1):
            k = sub * NSTEP + step
            d = d + jnp.concatenate([lower_ref[k, lev], upper_ref[k, lev]], axis=0)
            part = lat * d
            below = below_ref[sub * levels + lev, step : step + 1, :]
            below = jnp.where(bottom, below, pltpu.roll(part, rows - 1, 0))
            d = rest * d + below + east(lon * d)
        if sub == 0:
            earlier = earlier_ref[lev]
        else:
            earlier = jnp.concatenate(
                [end_low_ref[sub - 1, lev], end_high_ref[sub - 1, lev]], axis=0
            )
        g = ew * (inc_ref[sub, lev] - earlier) - d
        grad_ref[lev] = g
        for i in range(pairs):
            for which, ref in enumerate((step_ref, change_ref)):
                dots_ref[which * pairs + i] += fold(g * ref[i, sub, lev].astype(F32))
        return 0

    lax.fori_loop(0, levels, one, 0, unroll=2)


def second_kernel(last_ref, inc_ref, lat_ref, lon_ref, ew_ref, next_ref, *refs):
    step_ref, change_ref, grad_ref, dots_ref, acc_ref = refs[-5:]
    subs, levels, _, _ = inc_ref.shape
    dots_ref[...] = jnp.zeros_like(dots_ref)
    acc_ref[...] = jnp.zeros_like(acc_ref)

    def beside(lev):
        pair_products(step_ref, change_ref, acc_ref, (subs - 1) * levels + lev)

    add_gradient(
        subs - 1,
        last_ref,
        inc_ref,
        lat_ref,
        lon_ref,
        ew_ref,
        next_ref,
        None,
        *refs[:-3],
        grad_ref,
        dots_ref,
        beside,
    )


def first_kernel(inc_ref, lat_ref, lon_ref, ew_ref, previous_ref, *refs):
    dots_in, products_ref, grad_ref, stats_ref, dots_ref, acc_ref, gram_ref = refs[-7:]
    step_ref, change_ref = refs[-9:-7]
    pairs, _, _, rows, _ = step_ref.shape
    dots_ref[...] = dots_in[...]
    acc_ref[...] = products_ref[...]

    def beside(lev):
        pair_products(step_ref, change_ref, acc_ref, lev)

    add_gradient(
        0,
        None,
        inc_ref,
        lat_ref,
        lon_ref,
        ew_ref,
        None,
        previous_ref,
        *refs[:-7],
        grad_ref,
        dots_ref,
        beside,
    )
    pair_sums(acc_ref, rows, gram_ref)
    sums = [jnp.sum(dots_ref[v], axis=0, keepdims=True) for v in range(2 * pairs)]
    sums = jnp.concatenate(sums, axis=0)
    dots = jnp.sum(sums, axis=1, keepdims=True)
    row, group, inner = lane_places(gram_ref.shape)
    ahead = (group - row) % pairs
    moved = jnp.concatenate([dots[pairs:], dots[:pairs]], axis=0)
    out = jnp.where(ahead == WITH_CHANGE, dots, jnp.where(ahead == WITH_STEP, moved, gram_ref[...]))
    out = jnp.where(row < pairs, gram_ref[...], out)
    stats_ref[...] = jnp.sum(jnp.where(inner == row, out, 0.0), axis=0, keepdims=True)


def fold(x):
    longs = x.shape[1]
    whole = longs - longs % LANES
    x = x[:8] + x[8:]
    out = x[:, :LANES]
    for first in range(LANES, whole, LANES):
        out = out + x[:, first : first + LANES]
    if whole < longs:
        tail = jnp.concatenate(
            [x[:, whole:], jnp.zeros((8, LANES - (longs - whole)), F32)], axis=1
        )
        out = out + tail
    return out


def direction_kernel(
    stats_ref, first_ref, second_ref, step_ref, change_ref, grad_out, direction_out, coef_ref,
    out_ref, sems,
):
    pairs, subs, levels, _, _ = step_ref.shape
    both = 2 * pairs
    count = subs * levels
    grads = (first_ref, second_ref)
    handed = [
        pltpu.make_async_copy(ref, grad_out.at[sub], sems.at[count + sub])
        for sub, ref in enumerate(grads)
    ]
    for copy in handed:
        copy.start()
    stats = jnp.sum(stats_ref[...], axis=0, keepdims=True)
    shape = (both, LANES)
    row, group, inner = lane_places(shape)
    gram = jnp.broadcast_to(stats, shape)

    def column(mask, x):
        return jnp.sum(jnp.where(mask, x, 0.0), axis=1, keepdims=True)

    order = row % pairs
    changes = row >= pairs
    ahead = jnp.where(changes, WITH_CHANGE, WITH_STEP)
    dots = column((inner == pairs + order) & (group == (order + ahead) % pairs), gram)

    def with_change_of(c):
        swap = changes & ((c - order) % pairs >= WITH_CHANGE)
        return (group == jnp.where(swap, order, c)) & (inner == jnp.where(swap, pairs + c, row))

    by_change = [column(with_change_of(c), gram) for c in range(pairs)]
    by_step = [column((group == row) & (inner == i), gram)[:pairs] for i in range(pairs)]
    diagonal = column((group == row) & (inner == row), gram)[:pairs]
    rho = 1.0 / diagonal
    with_step, with_change = dots[:pairs], dots[pairs:]
    alphas = [None] * pairs
    for i in range(pairs - 1, -1, -1):
        alphas[i] = rho[i : i + 1] * with_step[i : i + 1]
        with_step = with_step - alphas[i] * by_change[i][:pairs]
        with_change = with_change - alphas[i] * by_change[i][pairs:]
    gamma = diagonal[pairs - 1 : pairs] / by_change[pairs - 1][both - 1 : both]
    with_change = gamma * with_change
    coef_ref[both] = jnp.broadcast_to(gamma, (8, LANES))
    for i in range(pairs):
        beta = rho[i : i + 1] * with_change[i : i + 1]
        rise = alphas[i] - beta
        with_change = with_change + rise * by_step[i]
        coef_ref[i] = jnp.broadcast_to(rise, (8, LANES))
        coef_ref[pairs + i] = jnp.broadcast_to(-gamma * alphas[i], (8, LANES))


    copies = []
    for sub in range(subs):
        for lev in range(levels):
            total = coef_ref[both][:1, :1] * grads[sub][lev]
            for i in range(pairs):
                total += coef_ref[i][:1, :1] * step_ref[i, sub, lev].astype(F32)
                total += coef_ref[pairs + i][:1, :1] * change_ref[i, sub, lev].astype(F32)
            out_ref[sub, lev] = total
            copies.append(
                pltpu.make_async_copy(
                    out_ref.at[sub, lev], direction_out.at[sub, lev], sems.at[len(copies)]
                )
            )
            copies[-1].start()
    for copy in copies + handed:
        copy.wait()


def on_device(
    increment,
    forcing,
    lat_courant,
    lon_courant,
    error_weight,
    site_index,
    site_count,
    site_value,
    site_weight,
    pair_step,
    pair_change,
):
    subs, levels, rows, longs = increment.shape
    pairs = pair_step.shape[0]
    slots = site_index.shape[2]
    count = subs * levels
    wide = -(-longs // LANES) * LANES
    devices = lax.axis_size("tm") * lax.axis_size("space")
    last = jnp.where(lax.axis_index("tm") == lax.axis_size("tm") - 1, 0.0, 1.0)
    last = last.astype(F32).reshape(1)

    def like(x):
        return pltpu.VMEM(x.shape, x.dtype)

    def floats(*shape):
        return pltpu.VMEM(shape, F32)

    def far(*arrays):
        return [pltpu.with_memory_space_constraint(x, pltpu.HBM) for x in arrays]

    arguments = (increment, forcing, lat_courant, lon_courant, site_index)
    following, edge, inc, push, lat, lon, index = pl.pallas_call(
        edge_kernel,
        in_specs=[FAR] * len(arguments),
        out_specs=[WHOLE] * (2 + len(arguments)),
        out_shape=[floats(levels, rows, longs), floats(count, NSTEP, longs)]
        + [like(x) for x in arguments],
        scratch_shapes=[pltpu.SemaphoreType.DMA((len(arguments) + 5,))],
        compiler_params=params(16),
        name="edge",
    )(*far(*arguments))
    above = shifted(edge, "space", 1)
    following = shifted(following, "tm", -1)

    row_shape = (subs * NSTEP, 1, slots)
    row_scratch = [
        pltpu.VMEM(row_shape, F32),
        pltpu.VMEM(row_shape, jnp.int32),
        pltpu.VMEM(row_shape, jnp.int32),
    ]
    rows_of_slots, end_high, steps, changes, ew = pl.pallas_call(
        inner_kernel,
        in_specs=[WHOLE] * 5 + [FAR] * 3,
        out_specs=[WHOLE] * 5,
        out_shape=[
            floats(3, subs * NSTEP, slots),
            floats(subs, levels, 8, longs),
            like(pair_step),
            like(pair_change),
            like(error_weight),
        ],
        scratch_shapes=[
            pltpu.VMEM((subs * NSTEP, levels, rows, wide), F32),
        ]
        + row_scratch
        + [pltpu.SemaphoreType.DMA((3, pairs))],
        compiler_params=params(28),
        name="inner",
    )(inc, push, lat, lon, index, *far(pair_step, pair_change, error_weight))

    end_low, sent, edge, part, dep = pl.pallas_call(
        outer_kernel,
        in_specs=[SCALAR] + [WHOLE] * 7 + [SCALAR] + [FAR] * 2 + [WHOLE] * 2,
        out_specs=[WHOLE] * 5,
        out_shape=[
            floats(subs, levels, 8, longs),
            floats(levels, rows, longs),
            floats(count, NSTEP, longs),
            floats(subs * NSTEP, levels, 8, longs),
            floats(subs * NSTEP, slots),
        ],
        scratch_shapes=[
            pltpu.VMEM((subs * NSTEP, levels, 8, wide), F32),
            pltpu.VMEM(site_value.shape, F32),
            pltpu.VMEM(site_value.shape, F32),
        ]
        + row_scratch
        + [pltpu.VMEM(row_shape, F32), pltpu.SemaphoreType.DMA((2,))],
        compiler_params=params(24),
        name="outer",
    )(
        last,
        inc,
        push,
        lat,
        lon,
        ew,
        following,
        above,
        site_count.reshape(subs, NSTEP),
        *far(site_value, site_weight),
        rows_of_slots,
        end_high,
    )
    previous = shifted(sent, "tm", 1)
    below = shifted(edge, "space", -1)

    lower, upper = pl.pallas_call(
        scatter_kernel,
        in_specs=[WHOLE] * 3,
        out_specs=[WHOLE] * 2,
        out_shape=[floats(subs * NSTEP, levels, 8, longs)] * 2,
        scratch_shapes=row_scratch[1:] + row_scratch[:1],
        compiler_params=params(24),
        cost_estimate=pl.CostEstimate(flops=6 * 10**9, bytes_accessed=1 << 20, transcendentals=0),
        name="scatter",
    )(rows_of_slots, dep, part)

    shared = (end_low, end_high, lower, upper, below, steps, changes)
    grad_second, dots, products = pl.pallas_call(
        second_kernel,
        in_specs=[SCALAR] + [WHOLE] * 12,
        out_specs=[WHOLE] * 3,
        out_shape=[
            floats(levels, rows, longs),
            floats(2 * pairs, 8, LANES),
            floats(pairs * rows, 2 * pairs * rows),
        ],
        compiler_params=params(16),
        name="second",
    )(last, inc, lat, lon, ew, following, *shared)
    grad_first, stats = pl.pallas_call(
        first_kernel,
        in_specs=[WHOLE] * 14,
        out_specs=[WHOLE] * 2,
        out_shape=[floats(levels, rows, longs), floats(1, LANES)],
        scratch_shapes=[
            pltpu.VMEM((2 * pairs, 8, LANES), F32),
            pltpu.VMEM(products.shape, F32),
            pltpu.VMEM((2 * pairs, pairs * rows), F32),
        ],
        compiler_params=params(16),
        name="first",
    )(inc, lat, lon, ew, previous, *shared, dots, products)

    stats = jnp.broadcast_to(stats[None], (devices,) + stats.shape)
    stats = lax.all_to_all(stats, ("tm", "space"), 0, 0).reshape(devices, LANES)

    return pl.pallas_call(
        direction_kernel,
        in_specs=[WHOLE] * 5,
        out_specs=[FAR] * 2,
        out_shape=[jax.ShapeDtypeStruct(increment.shape, F32)] * 2,
        scratch_shapes=[
            pltpu.VMEM((2 * pairs + 1, 8, LANES), F32),
            pltpu.VMEM(increment.shape, F32),
            pltpu.SemaphoreType.DMA((count + subs,)),
        ],
        compiler_params=params(16),
        name="direction",
    )(stats, grad_first, grad_second, steps, changes)


def solution(mesh):
    return jax.shard_map(
        on_device,
        mesh=mesh,
        in_specs=(
            P("tm", None, "space", None),
            P("tm", None, "space", None),
            P(None, "space", None),
            P(None, "space", None),
            P(None, "space", None),
            P("tm", None, "space"),
            P("tm", None, "space"),
            P("tm", None, "space"),
            P("tm", None, "space"),
            P(None, "tm", None, "space", None),
            P(None, "tm", None, "space", None),
        ),
        out_specs=(P("tm", None, "space", None), P("tm", None, "space", None)),
        check_vma=False,
    )
```
